256 devices in a mesh: band: 32 (over x, z_lo, core), dom: 8 (over y, z_hi).
Axes of the slice: x: 4, y: 4, z: 8 (z_hi: 2, z_lo: 4; z = z_hi * 4 + z_lo), core: 2. Of those that a mesh axis runs over, the one named last changes fastest.
Arguments:
- orbitals: bfloat16 [96, 64, 8192], P('dom', None, 'band'), may hold values from -19 to 19
- potential: bfloat16 [96, 64], replicated, may hold values from -1 to 0
- rot_first: bfloat16 [8192, 8192], P('dom', 'band'), may hold values from -0.0625 to 0.0625
- rot_second: bfloat16 [8192, 8192], P('dom', 'band'), may hold values from -0.0625 to 0.0625
Outputs:
- rotated: bfloat16 [96, 64, 8192], P('dom', None, 'band')
The draws below stay inside these ranges and needn't reach their ends.
All inputs are finite; a program needn't handle non-finite values.
Results may differ from the reference program's by a relative error of at most 0.0063.
Values may be sent and summed in bfloat16 or wider, within the bound.
A program may use at most 64 MiB of HBM per device.

```python
import jax
import jax.numpy as jnp
from jax import lax

NY = 64
NS = 8192
NX = 96


def draw_orbitals(key, part):
    key_base = jax.random.fold_in(key, 11)
    key_cell = jax.random.fold_in(key, 12)
    ramp = 1.0 + 2.0 * jnp.arange(NX, dtype=jnp.float32) / max(NX - 1, 1)
    cell = jax.random.uniform(key_cell, (NX, NY, 1), jnp.float32, 0.6, 1.4)
    base = jnp.clip(jax.random.normal(key_base, (NX, NY, NS), jnp.float32), -4.5, 4.5)
    return (base * cell * ramp[:, None, None]).astype(jnp.bfloat16)


def steps_of(own_key, extent, cuts, least, high):
    loudness = 1.0
    for position, shards_of in cuts:
        heights = jax.random.uniform(jax.random.fold_in(jax.random.fold_in(own_key, 6), position), (shards_of,), jnp.float32, least / len(cuts), high / len(cuts))
        loudness = loudness * jnp.repeat(jnp.exp(heights), extent[position] // shards_of).reshape((-1,) + (1,) * (len(extent) - 1 - position))
    return loudness


def scatter_about(rng, dims, spread, limit, shards=(), kind=jnp.bfloat16):
    gain = steps_of(rng, dims, shards, -0.22, 0.18) if shards else 1.0
    result = jax.random.normal(rng, dims, jnp.float32) * spread * gain
    return jnp.minimum(jnp.maximum(result, -limit), limit).astype(kind)


def setup_inputs(seed: int = 0) -> dict:
    key_list = jax.random.split(jax.random.key(seed), 5)
    return {
        "orbitals": draw_orbitals(jax.random.fold_in(key_list[4], 71), 0),
        "potential": jnp.clip(jax.random.uniform(key_list[1], (NX, NY), jnp.float32, -1.0, 0.0), -1.0, 0.0).astype(jnp.bfloat16),
        "rot_first": scatter_about(key_list[2], (NS, NS), NS ** -0.5, 0.0625, ((0, 8), (1, 32))),
        "rot_second": scatter_about(key_list[3], (NS, NS), NS ** -0.5, 0.0625, ((0, 8), (1, 32))),
    }


stencil_weights = (-5369.0 / 1800.0, 12.0 / 7.0, -15.0 / 56.0, 10.0 / 189.0, -1.0 / 112.0, 2.0 / 1925.0, -1.0 / 16632.0)
filter_center = 3.8
filter_half = 3.3

def hamiltonian(field, volts):
    padded = jnp.pad(field, ((6, 6), (6, 6), (0, 0)))
    width = field.shape[0]
    height = field.shape[1]
    lap = 2.0 * stencil_weights[0] * field
    for offset in range(1, 7):
        lap = lap + stencil_weights[offset] * (padded[6 + offset:6 + offset + width, 6:6 + height] + padded[6 - offset:6 - offset + width, 6:6 + height] + padded[6:6 + width, 6 + offset:6 + offset + height] + padded[6:6 + width, 6 - offset:6 - offset + height])
    return -0.5 * lap + volts[:, :, None] * field

def reference(orbitals, potential, rot_first, rot_second):
    volts = potential.astype(jnp.float32)
    start = orbitals.astype(jnp.float32)
    first_degree = ((hamiltonian(start, volts) - filter_center * start) / filter_half).astype(jnp.bfloat16)
    first_f = first_degree.astype(jnp.float32)
    filtered = (2.0 * (hamiltonian(first_f, volts) - filter_center * first_f) / filter_half - start).astype(jnp.bfloat16)
    flat = filtered.reshape(NX * NY, NS)
    turned = jnp.dot(flat, rot_first, preferred_element_type=jnp.float32)
    mean_square = lax.optimization_barrier(jnp.sum(turned * turned, axis=0)) / (NX * NY)
    normed = (turned / jnp.sqrt(mean_square + 1e-06)[None, :]).astype(jnp.bfloat16)
    rotated = jnp.dot(normed, rot_second, preferred_element_type=jnp.float32).astype(jnp.bfloat16)
    return rotated.reshape(NX, NY, NS)
```

```python
import functools

import jax
import jax.numpy as jnp
from jax import lax
from jax.experimental import pallas as pl
from jax.experimental.pallas import tpu as pltpu
from jax.sharding import PartitionSpec as P

stencil_weights = (
    -5369.0 / 1800.0,
    12.0 / 7.0,
    -15.0 / 56.0,
    10.0 / 189.0,
    -1.0 / 112.0,
    2.0 / 1925.0,
    -1.0 / 16632.0,
)
filter_center = 3.8
filter_half = 3.3

MESH = pl.DeviceIdType.MESH
GRID_X = 96
NY = 64
OWN = 12
ROWS = OWN * NY
LANES = 256
HALF = 128
CHUNKS = 3
CROWS = ROWS // CHUNKS
PAIR = 2 * OWN
EXT = PAIR + 12
CELLS = GRID_X * NY


def aligned(value, multiple):
    return pl.multiple_of(value, multiple)


def kernel(
    orb, pot, r1, r2, out,
    oext, dext, vpad, volt, filt, g1, g2, rb1, rb2, pbuf, prec, tq, sq,
    swap_s, swap_r, back_s, back_r, loc, halo_s, halo_r,
    g_s, g_r, p_s, p_r, sq_s, sq_r, rz_s, rz_r, ry_s, ry_r,
):
    band = lax.axis_index("band")
    dom = lax.axis_index("dom")
    x = band // 8
    zl = (band // 2) % 4
    za = zl // 2
    zb = zl % 2
    core = band % 2
    y = dom // 2
    zh = dom % 2

    def device(x_=None, y_=None, zh_=None, za_=None, zb_=None, core_=None):
        pick = lambda new, old: old if new is None else new
        b = pick(x_, x) * 8 + (pick(za_, za) * 2 + pick(zb_, zb)) * 2 + pick(core_, core)
        d = pick(y_, y) * 2 + pick(zh_, zh)
        return {"band": b, "dom": d}

    def around(value, step):
        return (value + step) % 4

    def remote(src, dst, send, recv, to):
        return pltpu.make_async_remote_copy(
            src_ref=src, dst_ref=dst, send_sem=send, recv_sem=recv, device_id=to, device_id_type=MESH
        )

    barrier = pltpu.get_barrier_semaphore()
    partners = []
    for step in range(1, 8):
        z = (zh * 4 + zl + step) % 8
        partners.append(device(zh_=z // 4, za_=(z // 2) % 2, zb_=z % 2))
    for step in range(1, 4):
        partners.append(device(x_=around(x, step)))
        partners.append(device(y_=around(y, step)))
        partners.append(device(y_=around(y, step), zh_=1 - zh))
    partners.append(device(core_=1 - core))
    for to in partners:
        pl.semaphore_signal(barrier, inc=1, device_id=to, device_id_type=MESH)
    pl.semaphore_wait(barrier, len(partners))

    mine = aligned(zh * HALF, HALF)
    theirs = aligned((1 - zh) * HALF, HALF)
    own_at = aligned((6 + OWN * zh) * NY, NY)
    partner_at = aligned((6 + OWN * (1 - zh)) * NY, NY)
    swap = remote(
        orb.at[:, pl.ds(theirs, HALF)], oext.at[pl.ds(own_at, ROWS)], swap_s, swap_r, device(zh_=1 - zh)
    )
    swap.start()
    keep = pltpu.make_async_copy(orb.at[:, pl.ds(mine, HALF)], oext.at[pl.ds(own_at, ROWS)], loc.at[0])
    keep.start()

    def coef_z(i, r, rb):
        rows = pl.ds(aligned(y * 1024, 1024), 1024)
        here = rb.at[za, rows]
        other = remote(r, here, rz_s.at[i, 0], rz_r.at[i, za], device(zh_=1 - zh, za_=zh))
        near = remote(r, here, rz_s.at[i, 1], rz_r.at[i, za], device(za_=zh))
        own = pltpu.make_async_copy(r, here, rz_r.at[i, za])
        return other, near, own

    def coef_z_start(i, r, rb):
        other, near, own = coef_z(i, r, rb)
        other.start()

        @pl.when(za != zh)
        def _():
            near.start()

        @pl.when(za == zh)
        def _():
            own.start()

    def coef_y(i, rb, part):
        rows = pl.ds(aligned(y * 1024, 1024), 1024)
        return [
            remote(
                rb.at[part, rows], rb.at[part, rows], ry_s.at[i, part, step - 1], ry_r.at[i, part, step - 1],
                device(y_=around(y, step)),
            )
            for step in (1, 3, 2)
        ]

    def coef_y_start(i, r, rb):
        for part in range(2):
            pltpu.make_async_copy(r, rb.at[part, pl.ds(aligned(y * 1024, 1024), 1024)], rz_r.at[i, part]).wait()
            for copy in coef_y(i, rb, part):
                copy.start()

    def coef_wait(i, rb):
        for part in range(2):
            for copy in coef_y(i, rb, part):
                copy.wait_recv()

    def coef_end(i, r, rb):
        other, near, own = coef_z(i, r, rb)
        other.wait_send()

        @pl.when(za != zh)
        def _():
            near.wait_send()

        for part in range(2):
            for copy in coef_y(i, rb, part):
                copy.wait_send()

    coef_z_start(0, r1, rb1)

    diagonal = lax.broadcasted_iota(jnp.int32, (NY, NY), 0) == lax.broadcasted_iota(jnp.int32, (NY, NY), 1)
    ones = jnp.ones((NY, HALF), jnp.bfloat16)

    def spread(i, carry):
        row = pot[pl.ds(y * PAIR + i, 1), :]
        square = jnp.where(diagonal, jnp.broadcast_to(row, (NY, NY)), 0.0).astype(jnp.bfloat16)
        volt[i] = jnp.dot(square, ones, preferred_element_type=jnp.float32)
        return carry

    lax.fori_loop(0, PAIR, spread, 0)

    def clear(i, carry):
        vpad[i, 0:8, :] = jnp.zeros((8, HALF), jnp.float32)
        vpad[i, 72:80, :] = jnp.zeros((8, HALF), jnp.float32)
        return carry

    lax.fori_loop(0, EXT, clear, 0)

    def rims(i, ext):
        up = remote(
            ext.at[pl.ds(24 * NY, 6 * NY)], ext.at[pl.ds(0, 6 * NY)], halo_s.at[i, 0], halo_r.at[i, 0],
            device(y_=around(y, 1)),
        )
        down = remote(
            ext.at[pl.ds(6 * NY, 6 * NY)], ext.at[pl.ds(30 * NY, 6 * NY)], halo_s.at[i, 1], halo_r.at[i, 1],
            device(y_=around(y, 3)),
        )
        return up, down

    def widen(ext, first, count, keep_it):
        def step(i, carry):
            at = first + i
            value = ext[pl.ds(aligned(at * NY, NY), NY), :].astype(jnp.float32)
            if keep_it is not None:
                value = jnp.where(keep_it, value, 0.0)
            vpad[at, 8:72, :] = value
            return carry

        lax.fori_loop(0, count, step, 0)

    def applied(i):
        center = vpad[i + 6, 8:72, :]
        lap = 2.0 * stencil_weights[0] * center
        for k in range(1, 7):
            lap = lap + stencil_weights[k] * (
                (vpad[i + 6 + k, 8:72, :] + vpad[i + 6 - k, 8:72, :])
                + (vpad[i + 6, 8 + k : 72 + k, :] + vpad[i + 6, 8 - k : 72 - k, :])
            )
        return -0.5 * lap + volt[i] * center, center

    def field(i, ext):
        for copy in rims(i, ext):
            copy.start()
        widen(ext, 6, PAIR, None)
        for copy in rims(i, ext):
            copy.wait_recv()
        widen(ext, 0, 6, y > 0)
        widen(ext, 30, 6, y < 3)

    keep.wait()
    swap.wait_recv()
    field(0, oext)

    def first(i, carry):
        value, center = applied(i)
        dext[pl.ds(aligned((i + 6) * NY, NY), NY), :] = (
            (value - filter_center * center) * (1.0 / filter_half)
        ).astype(jnp.bfloat16)
        return carry

    lax.fori_loop(0, PAIR, first, 0)
    field(1, dext)

    def second(i, carry):
        value, center = applied(i)
        start = oext[pl.ds(aligned((i + 6) * NY, NY), NY), :].astype(jnp.float32)
        filt[pl.ds(aligned(i * NY, NY), NY), :] = (
            (value - filter_center * center) * (2.0 / filter_half) - start
        ).astype(jnp.bfloat16)
        return carry

    own_slot = (x * 2 + zb) * 2 + core
    half_lanes = pl.ds(mine, HALF)

    def back(j):
        source = filt.at[pl.ds(aligned((1 - zh) * ROWS + j * CROWS, CROWS), CROWS)]
        place = g1.at[own_slot, pl.ds(j * CROWS, CROWS), half_lanes]
        return remote(source, place, back_s.at[j], back_r.at[j], device(zh_=1 - zh))

    def stay(j):
        source = filt.at[pl.ds(aligned(zh * ROWS + j * CROWS, CROWS), CROWS)]
        place = g1.at[own_slot, pl.ds(j * CROWS, CROWS), half_lanes]
        return pltpu.make_async_copy(source, place, loc.at[1 + j])

    per = OWN // CHUNKS
    for j in range(CHUNKS):
        lax.fori_loop((1 - zh) * OWN + j * per, (1 - zh) * OWN + (j + 1) * per, second, 0)
        back(j).start()
    for j in range(CHUNKS):
        lax.fori_loop(zh * OWN + j * per, zh * OWN + (j + 1) * per, second, 0)
        stay(j).start()

    other_core = device(core_=1 - core)

    def block(g, slot, j):
        return g.at[slot, pl.ds(aligned(j * CROWS, CROWS), CROWS)]

    def send(i, g, slot, j, n, to):
        return remote(block(g, slot, j), block(g, slot, j), g_s.at[i, j, n], g_r.at[i, j, slot], to)

    def own_sends(i, g, j):
        places = [device(zb_=1 - zb), device(x_=around(x, 1)), device(x_=around(x, 3)), device(x_=around(x, 2)), other_core]
        return [send(i, g, own_slot, j, n, to) for n, to in enumerate(places)]

    def pair_sends(i, g, j):
        slot = (x * 2 + 1 - zb) * 2 + core
        places = [device(x_=around(x, 1)), device(x_=around(x, 3)), device(x_=around(x, 2)), other_core]
        return [send(i, g, slot, j, 5 + n, to) for n, to in enumerate(places)]

    def far_sends(i, g, j):
        sends = []
        for step in (1, 3, 2):
            for b in (0, 1):
                slot = (around(x, step) * 2 + b) * 2 + core
                sends.append(send(i, g, slot, j, 9 + len(sends), other_core))
        return sends

    def arrived(i, g, slot, j):
        send(i, g, slot, j, 0, other_core).wait_recv()

    def gather_own(i, g, j):
        for copy in own_sends(i, g, j):
            copy.start()

    def gather_pair(i, g, j):
        arrived(i, g, (x * 2 + 1 - zb) * 2 + core, j)
        for copy in pair_sends(i, g, j):
            copy.start()

    def gather_far(i, g, j):
        for copy in far_sends(i, g, j):
            copy.wait_recv()
            copy.start()
        for slot in range(8):
            arrived(i, g, slot * 2 + 1 - core, j)

    def gather_end(i, g):
        def step(j, carry):
            for copy in own_sends(i, g, j) + pair_sends(i, g, j) + far_sends(i, g, j):
                copy.wait_send()
            return carry

        lax.fori_loop(0, CHUNKS, step, 0)

    def product(g, rb, j, part):
        rows = pl.ds(aligned(j * CROWS, CROWS), CROWS)
        total = None
        for slot in range(16):
            term = jnp.dot(
                g[slot, rows, :], rb[part, slot * LANES : (slot + 1) * LANES, :], preferred_element_type=jnp.float32
            )
            total = term if total is None else total + term
        return total

    def partial_send(i, j):
        return remote(pbuf.at[i, j], prec.at[i, j], p_s.at[i, j], p_r.at[i, j], device(za_=1 - za))

    def rotate(i, g, rb):
        def step(j, carry):
            gather_far(i, g, j)
            pbuf[i, j] = product(g, rb, j, 1 - za).astype(jnp.bfloat16)
            partial_send(i, j).start()
            tq[j] = product(g, rb, j, za)
            return carry

        lax.fori_loop(0, CHUNKS, step, 0)

    coef_y_start(0, r1, rb1)
    coef_z_start(1, r2, rb2)
    for j in range(CHUNKS):
        stay(j).wait()
        back(j).wait_recv()
        gather_own(0, g1, j)
    for j in range(CHUNKS):
        gather_pair(0, g1, j)
    coef_wait(0, rb1)
    rotate(0, g1, rb1)
    coef_y_start(1, r2, rb2)

    sums = jnp.zeros((8, LANES), jnp.float32)
    for j in range(CHUNKS):
        partial_send(0, j).wait_recv()

        def squares(n, total):
            rows = pl.ds(aligned(n * 32, 32), 32)
            value = tq[j, rows, :] + prec[0, j, rows, :].astype(jnp.float32)
            tq[j, rows, :] = value
            return total + jnp.sum((value * value).reshape(4, 8, LANES), axis=0)

        sums = lax.fori_loop(0, CROWS // 32, squares, sums)
    sq[dom] = sums

    def share(step):
        to = (dom + step) % 8
        return remote(sq.at[dom], sq.at[dom], sq_s.at[step - 1], sq_r.at[step - 1], {"band": band, "dom": to})

    for step in range(1, 8):
        share(step).start()
    for step in range(1, 8):
        share(step).wait_recv()
    total = sq[0]
    for d in range(1, 8):
        total = total + sq[d]
    mean_square = jnp.sum(total, axis=0, keepdims=True) * (1.0 / CELLS)
    scale = 1.0 / jnp.sqrt(mean_square + 1e-06)
    for j in range(CHUNKS):

        def normalize(n, carry):
            rows = pl.ds(aligned(n * 32, 32), 32)
            g2[own_slot, pl.ds(aligned(j * CROWS + n * 32, 32), 32), :] = (tq[j, rows, :] * scale).astype(jnp.bfloat16)
            return carry

        lax.fori_loop(0, CROWS // 32, normalize, 0)
        gather_own(1, g2, j)

    for j in range(CHUNKS):
        gather_pair(1, g2, j)
    coef_wait(1, rb2)
    rotate(1, g2, rb2)

    for j in range(CHUNKS):
        partial_send(1, j).wait_recv()

        def finish(n, carry):
            rows = pl.ds(aligned(n * 32, 32), 32)
            out[pl.ds(aligned(j * CROWS + n * 32, 32), 32), :] = (
                tq[j, rows, :] + prec[1, j, rows, :].astype(jnp.float32)
            ).astype(jnp.bfloat16)
            return carry

        lax.fori_loop(0, CROWS // 32, finish, 0)

    swap.wait_send()
    for j in range(CHUNKS):
        back(j).wait_send()
    for i, ext in ((0, oext), (1, dext)):
        for copy in rims(i, ext):
            copy.wait_send()
    for i, (g, r, rb) in enumerate(((g1, r1, rb1), (g2, r2, rb2))):
        gather_end(i, g)
        coef_end(i, r, rb)
        for j in range(CHUNKS):
            partial_send(i, j).wait_send()
    for step in range(1, 8):
        share(step).wait_send()


def shards(orbitals, potential, rot_first, rot_second):
    bf16, f32 = jnp.bfloat16, jnp.float32
    vmem = pl.BlockSpec(memory_space=pltpu.VMEM)
    dma = pltpu.SemaphoreType.DMA
    result = pl.pallas_call(
        kernel,
        out_shape=jax.ShapeDtypeStruct((ROWS, LANES), bf16),
        in_specs=[vmem] * 4,
        out_specs=vmem,
        scratch_shapes=[
            pltpu.VMEM((EXT * NY, HALF), bf16),
            pltpu.VMEM((EXT * NY, HALF), bf16),
            pltpu.VMEM((EXT, NY + 16, HALF), f32),
            pltpu.VMEM((PAIR, NY, HALF), f32),
            pltpu.VMEM((PAIR * NY, HALF), bf16),
            pltpu.VMEM((16, ROWS, LANES), bf16),
            pltpu.VMEM((16, ROWS, LANES), bf16),
            pltpu.VMEM((2, 4096, LANES), bf16),
            pltpu.VMEM((2, 4096, LANES), bf16),
            pltpu.VMEM((2, CHUNKS, CROWS, LANES), bf16),
            pltpu.VMEM((2, CHUNKS, CROWS, LANES), bf16),
            pltpu.VMEM((CHUNKS, CROWS, LANES), f32),
            pltpu.VMEM((8, 8, LANES), f32),
            dma, dma,
            dma((CHUNKS,)), dma((CHUNKS,)),
            dma((1 + CHUNKS,)),
            dma((2, 2)), dma((2, 2)),
            dma((2, CHUNKS, 15)), dma((2, CHUNKS, 16)),
            dma((2, CHUNKS)), dma((2, CHUNKS)),
            dma((7,)), dma((7,)),
            dma((2, 2)), dma((2, 2)),
            dma((2, 2, 3)), dma((2, 2, 3)),
        ],
        compiler_params=pltpu.CompilerParams(
            collective_id=0, has_side_effects=True, vmem_limit_bytes=56 << 20
        ),
    )(orbitals.reshape(ROWS, LANES), potential.astype(f32), rot_first, rot_second)
    return result.reshape(OWN, NY, LANES)


def solution(mesh):
    placed = (P("dom", None, "band"), P(), P("dom", "band"), P("dom", "band"))
    return jax.shard_map(
        shards, mesh=mesh, in_specs=placed, out_specs=P("dom", None, "band"), check_vma=False
    )
```

```python
import functools

import jax
import jax.numpy as jnp
from jax import lax
from jax.experimental import pallas as pl
from jax.experimental.pallas import tpu as pltpu
from jax.sharding import PartitionSpec as P

stencil_weights = (
    -5369.0 / 1800.0,
    12.0 / 7.0,
    -15.0 / 56.0,
    10.0 / 189.0,
    -1.0 / 112.0,
    2.0 / 1925.0,
    -1.0 / 16632.0,
)
filter_center = 3.8
filter_half = 3.3

MESH = pl.DeviceIdType.MESH
GRID_X = 96
NY = 64
OWN = 12
ROWS = OWN * NY
LANES = 256
HALF = 128
CHUNKS = 3
CROWS = ROWS // CHUNKS
PAIR = 2 * OWN
EXT = PAIR + 12
CELLS = GRID_X * NY
PIECES = 2
PROWS = 1024 // PIECES


def aligned(value, multiple):
    return pl.multiple_of(value, multiple)


def kernel(
    orb, pot, r1, r2, out,
    oext, dext, vpad, potf, volt, filt, g1, g2, rb1, rb2, pbuf, prec, tq, sq,
    swap_s, swap_r, back_s, back_r, loc, halo_s, halo_r,
    g_s, g_r, p_s, p_r, sq_s, sq_r, rz_s, rz_r, ry_s, ry_r,
):
    band = lax.axis_index("band")
    dom = lax.axis_index("dom")
    x = band // 8
    zl = (band // 2) % 4
    za = zl // 2
    zb = zl % 2
    core = band % 2
    y = dom // 2
    zh = dom % 2

    def device(x_=None, y_=None, zh_=None, za_=None, zb_=None, core_=None):
        pick = lambda new, old: old if new is None else new
        b = pick(x_, x) * 8 + (pick(za_, za) * 2 + pick(zb_, zb)) * 2 + pick(core_, core)
        d = pick(y_, y) * 2 + pick(zh_, zh)
        return {"band": b, "dom": d}

    def around(value, step):
        return (value + step) % 4

    def remote(src, dst, send, recv, to):
        return pltpu.make_async_remote_copy(
            src_ref=src, dst_ref=dst, send_sem=send, recv_sem=recv, device_id=to, device_id_type=MESH
        )

    barrier = pltpu.get_barrier_semaphore()
    partners = []
    for step in range(1, 8):
        z = (zh * 4 + zl + step) % 8
        partners.append(device(zh_=z // 4, za_=(z // 2) % 2, zb_=z % 2))
    for step in range(1, 4):
        partners.append(device(x_=around(x, step)))
        partners.append(device(y_=around(y, step)))
        partners.append(device(y_=around(y, step), zh_=1 - zh))
    partners.append(device(core_=1 - core))
    for to in partners:
        pl.semaphore_signal(barrier, inc=1, device_id=to, device_id_type=MESH)
    pl.semaphore_wait(barrier, len(partners))

    mine = aligned(zh * HALF, HALF)
    theirs = aligned((1 - zh) * HALF, HALF)
    own_at = aligned((6 + OWN * zh) * NY, NY)
    partner_at = aligned((6 + OWN * (1 - zh)) * NY, NY)
    swap = remote(
        orb.at[:, pl.ds(theirs, HALF)], oext.at[pl.ds(own_at, ROWS)], swap_s, swap_r, device(zh_=1 - zh)
    )
    swap.start()
    keep = pltpu.make_async_copy(orb.at[:, pl.ds(mine, HALF)], oext.at[pl.ds(own_at, ROWS)], loc.at[0])
    keep.start()

    def piece(q):
        return pl.ds(q * PROWS, PROWS)

    def slot_rows(step, q, first=0, count=PROWS):
        return pl.ds(aligned(around(y, step) * 1024 + q * PROWS + first, 128), count)

    def coef_z(i, r, rb, q):
        here = rb.at[za, slot_rows(0, q)]
        other = remote(r.at[piece(q)], here, rz_s.at[i, q, 0], rz_r.at[i, q, za], device(zh_=1 - zh, za_=zh))
        near = remote(r.at[piece(q)], here, rz_s.at[i, q, 1], rz_r.at[i, q, za], device(za_=zh))
        own = pltpu.make_async_copy(r.at[piece(q)], here, rz_r.at[i, q, za])
        return other, near, own

    def coef_z_start(i, r, rb):
        for q in range(PIECES):
            other, near, own = coef_z(i, r, rb, q)
            other.start()

            @pl.when(za != zh)
            def _():
                near.start()

            @pl.when(za == zh)
            def _():
                own.start()

    def ring(i, rb, part, q, n, step, to, first=0, count=PROWS):
        rows = slot_rows(step, q, first, count)
        return remote(
            rb.at[part, rows], rb.at[part, rows], ry_s.at[i, part, q, n], ry_r.at[i, part, q, n],
            device(y_=around(y, to)),
        )

    def coef_near(i, rb, q):
        return [ring(i, rb, part, q, n, 0, to) for part in range(2) for n, to in ((0, 1), (1, 3))]

    def coef_far(i, rb, q):
        half = PROWS // 2
        return [
            ring(i, rb, part, q, n, step, to, first, half)
            for part in range(2)
            for n, step, to, first in ((2, 3, 1, 0), (3, 1, 3, half))
        ]

    def coef_near_start(i, r, rb, q):
        for part in range(2):
            pltpu.make_async_copy(r.at[piece(q)], rb.at[part, slot_rows(0, q)], rz_r.at[i, q, part]).wait()
        for copy in coef_near(i, rb, q):
            copy.start()

    def coef_far_start(i, rb, q):
        for copy in coef_near(i, rb, q):
            copy.wait_recv()
        for copy in coef_far(i, rb, q):
            copy.start()

    def coef_wait(i, rb):
        for q in range(PIECES):
            for copy in coef_far(i, rb, q):
                copy.wait_recv()

    def coef_end(i, r, rb):
        for q in range(PIECES):
            other, near, own = coef_z(i, r, rb, q)
            other.wait_send()

            @pl.when(za != zh)
            def _():
                near.wait_send()

            for copy in coef_near(i, rb, q) + coef_far(i, rb, q):
                copy.wait_send()

    coef_z_start(0, r1, rb1)

    diagonal = lax.broadcasted_iota(jnp.int32, (NY, NY), 0) == lax.broadcasted_iota(jnp.int32, (NY, NY), 1)
    ones = jnp.ones((NY, HALF), jnp.bfloat16)

    potf[...] = pot[...].astype(jnp.float32)

    def spread(i, carry):
        row = potf[pl.ds(y * PAIR + i, 1), :]
        square = jnp.where(diagonal, jnp.broadcast_to(row, (NY, NY)), 0.0).astype(jnp.bfloat16)
        volt[i] = jnp.dot(square, ones, preferred_element_type=jnp.float32)
        return carry

    lax.fori_loop(0, PAIR, spread, 0)

    def clear(i, carry):
        vpad[i, 0:8, :] = jnp.zeros((8, HALF), jnp.float32)
        vpad[i, 72:80, :] = jnp.zeros((8, HALF), jnp.float32)
        return carry

    lax.fori_loop(0, EXT, clear, 0)

    def rims(i, ext):
        up = remote(
            ext.at[pl.ds(24 * NY, 6 * NY)], ext.at[pl.ds(0, 6 * NY)], halo_s.at[i, 0], halo_r.at[i, 0],
            device(y_=around(y, 1)),
        )
        down = remote(
            ext.at[pl.ds(6 * NY, 6 * NY)], ext.at[pl.ds(30 * NY, 6 * NY)], halo_s.at[i, 1], halo_r.at[i, 1],
            device(y_=around(y, 3)),
        )
        return up, down

    def widen(ext, first, count, keep_it):
        def step(i, carry):
            at = first + i
            value = ext[pl.ds(aligned(at * NY, NY), NY), :].astype(jnp.float32)
            if keep_it is not None:
                value = jnp.where(keep_it, value, 0.0)
            vpad[at, 8:72, :] = value
            return carry

        lax.fori_loop(0, count, step, 0)

    def applied(i):
        center = vpad[i + 6, 8:72, :]
        lap = 2.0 * stencil_weights[0] * center
        for k in range(1, 7):
            lap = lap + stencil_weights[k] * (
                (vpad[i + 6 + k, 8:72, :] + vpad[i + 6 - k, 8:72, :])
                + (vpad[i + 6, 8 + k : 72 + k, :] + vpad[i + 6, 8 - k : 72 - k, :])
            )
        return -0.5 * lap + volt[i] * center, center

    def field(i, ext):
        for copy in rims(i, ext):
            copy.start()
        coef_near_start(0, r1, rb1, i)
        widen(ext, 6, PAIR, None)
        for copy in rims(i, ext):
            copy.wait_recv()
        widen(ext, 0, 6, y > 0)
        widen(ext, 30, 6, y < 3)

    keep.wait()
    swap.wait_recv()
    field(0, oext)

    def first(i, carry):
        value, center = applied(i)
        dext[pl.ds(aligned((i + 6) * NY, NY), NY), :] = (
            (value - filter_center * center) * (1.0 / filter_half)
        ).astype(jnp.bfloat16)
        return carry

    lax.fori_loop(0, PAIR, first, 0)
    field(1, dext)

    def second(i, carry):
        value, center = applied(i)
        start = oext[pl.ds(aligned((i + 6) * NY, NY), NY), :].astype(jnp.float32)
        filt[pl.ds(aligned(i * NY, NY), NY), :] = (
            (value - filter_center * center) * (2.0 / filter_half) - start
        ).astype(jnp.bfloat16)
        return carry

    own_slot = (x * 2 + zb) * 2 + core
    half_lanes = pl.ds(mine, HALF)

    def back(j):
        source = filt.at[pl.ds(aligned((1 - zh) * ROWS + j * CROWS, CROWS), CROWS)]
        place = g1.at[own_slot, pl.ds(j * CROWS, CROWS), half_lanes]
        return remote(source, place, back_s.at[j], back_r.at[j], device(zh_=1 - zh))

    def stay(j):
        source = filt.at[pl.ds(aligned(zh * ROWS + j * CROWS, CROWS), CROWS)]
        place = g1.at[own_slot, pl.ds(j * CROWS, CROWS), half_lanes]
        return pltpu.make_async_copy(source, place, loc.at[1 + j])

    per = OWN // CHUNKS
    for j in range(CHUNKS):
        lax.fori_loop((1 - zh) * OWN + j * per, (1 - zh) * OWN + (j + 1) * per, second, 0)
        back(j).start()
    for j in range(CHUNKS):
        lax.fori_loop(zh * OWN + j * per, zh * OWN + (j + 1) * per, second, 0)
        stay(j).start()

    other_core = device(core_=1 - core)

    def block(g, slot, j):
        return g.at[slot, pl.ds(aligned(j * CROWS, CROWS), CROWS)]

    def send(i, g, slot, j, n, to):
        return remote(block(g, slot, j), block(g, slot, j), g_s.at[i, j, n], g_r.at[i, j, slot], to)

    right, left = device(x_=around(x, 1)), device(x_=around(x, 3))

    def slot_at(step, b):
        return (around(x, step) * 2 + b) * 2 + core

    def own_sends(i, g, j):
        return [send(i, g, own_slot, j, n, to) for n, to in enumerate((device(zb_=1 - zb), right, left, other_core))]

    def pair_sends(i, g, j):
        return [send(i, g, slot_at(0, 1 - zb), j, 4 + n, to) for n, to in enumerate((right, left, other_core))]

    def near_sends(i, g, j):
        sends = []
        for step, first, to in ((3, 0, right), (1, CROWS // 2, left)):
            for b in (0, 1):
                slot = slot_at(step, b)
                rows = pl.ds(aligned(j * CROWS + first, CROWS // 2), CROWS // 2)
                part = g.at[slot, rows]
                n = 7 + len(sends)
                sends.append(remote(part, part, g_s.at[i, j, n], g_r.at[i, j, slot], to))
                sends.append(send(i, g, slot, j, n + 1, other_core))
        return sends

    def far_sends(i, g, j):
        return [send(i, g, slot_at(2, b), j, 15 + b, other_core) for b in (0, 1)]

    def arrived(i, g, slot, j):
        send(i, g, slot, j, 0, other_core).wait_recv()

    def gather_own(i, g, j):
        for copy in own_sends(i, g, j):
            copy.start()

    def gather_pair(i, g, j):
        arrived(i, g, slot_at(0, 1 - zb), j)
        for copy in pair_sends(i, g, j):
            copy.start()

    def gather_near(i, g, j):
        for step in (3, 1):
            for b in (0, 1):
                arrived(i, g, slot_at(step, b), j)
        for copy in near_sends(i, g, j):
            copy.start()

    def gather_far(i, g, j):
        for b in (0, 1):
            arrived(i, g, slot_at(2, b), j)
        for copy in far_sends(i, g, j):
            copy.start()
        for slot in range(8):
            arrived(i, g, slot * 2 + 1 - core, j)

    def gather_end(i, g):
        def step(j, carry):
            for copy in own_sends(i, g, j) + pair_sends(i, g, j) + near_sends(i, g, j) + far_sends(i, g, j):
                copy.wait_send()
            return carry

        lax.fori_loop(0, CHUNKS, step, 0)

    def product(g, rb, j, part):
        rows = pl.ds(aligned(j * CROWS, CROWS), CROWS)
        total = None
        for slot in range(16):
            term = jnp.dot(
                g[slot, rows, :], rb[part, slot * LANES : (slot + 1) * LANES, :], preferred_element_type=jnp.float32
            )
            total = term if total is None else total + term
        return total

    def partial_send(i, j):
        return remote(pbuf.at[i, j], prec.at[i, j], p_s.at[i, j], p_r.at[i, j], device(za_=1 - za))

    def multiply(i, g, rb, j):
        gather_far(i, g, j)
        pbuf[i, j] = product(g, rb, j, 1 - za).astype(jnp.bfloat16)
        partial_send(i, j).start()
        tq[j] = product(g, rb, j, za)

    coef_far_start(0, rb1, 0)
    for j in range(CHUNKS):
        stay(j).wait()
        back(j).wait_recv()
        gather_own(0, g1, j)
    coef_far_start(0, rb1, 1)
    for j in range(CHUNKS):
        gather_pair(0, g1, j)
    coef_z_start(1, r2, rb2)
    gather_near(0, g1, 0)
    gather_near(0, g1, 1)
    coef_wait(0, rb1)
    multiply(0, g1, rb1, 0)
    gather_near(0, g1, 2)
    multiply(0, g1, rb1, 1)
    coef_near_start(1, r2, rb2, 0)
    multiply(0, g1, rb1, 2)
    coef_near_start(1, r2, rb2, 1)

    sums = jnp.zeros((8, LANES), jnp.float32)
    for j in range(CHUNKS):
        partial_send(0, j).wait_recv()

        def squares(n, total):
            rows = pl.ds(aligned(n * 32, 32), 32)
            value = tq[j, rows, :] + prec[0, j, rows, :].astype(jnp.float32)
            tq[j, rows, :] = value
            return total + jnp.sum((value * value).reshape(4, 8, LANES), axis=0)

        sums = lax.fori_loop(0, CROWS // 32, squares, sums)
    sq[dom] = sums

    def share(step):
        to = (dom + step) % 8
        return remote(sq.at[dom], sq.at[dom], sq_s.at[step - 1], sq_r.at[step - 1], {"band": band, "dom": to})

    for step in range(1, 8):
        share(step).start()
    for step in range(1, 8):
        share(step).wait_recv()
    total = sq[0]
    for d in range(1, 8):
        total = total + sq[d]
    mean_square = jnp.sum(total, axis=0, keepdims=True) * (1.0 / CELLS)
    scale = 1.0 / jnp.sqrt(mean_square + 1e-06)
    for j in range(CHUNKS):

        def normalize(n, carry):
            rows = pl.ds(aligned(n * 32, 32), 32)
            g2[own_slot, pl.ds(aligned(j * CROWS + n * 32, 32), 32), :] = (tq[j, rows, :] * scale).astype(jnp.bfloat16)
            return carry

        lax.fori_loop(0, CROWS // 32, normalize, 0)
        gather_own(1, g2, j)

    coef_far_start(1, rb2, 0)
    for j in range(CHUNKS):
        gather_pair(1, g2, j)
    coef_far_start(1, rb2, 1)
    gather_near(1, g2, 0)
    gather_near(1, g2, 1)
    coef_wait(1, rb2)
    multiply(1, g2, rb2, 0)
    gather_near(1, g2, 2)
    multiply(1, g2, rb2, 1)
    multiply(1, g2, rb2, 2)

    for j in range(CHUNKS):
        partial_send(1, j).wait_recv()

        def finish(n, carry):
            rows = pl.ds(aligned(n * 32, 32), 32)
            out[pl.ds(aligned(j * CROWS + n * 32, 32), 32), :] = (
                tq[j, rows, :] + prec[1, j, rows, :].astype(jnp.float32)
            ).astype(jnp.bfloat16)
            return carry

        lax.fori_loop(0, CROWS // 32, finish, 0)

    swap.wait_send()
    for j in range(CHUNKS):
        back(j).wait_send()
    for i, ext in ((0, oext), (1, dext)):
        for copy in rims(i, ext):
            copy.wait_send()
    for i, (g, r, rb) in enumerate(((g1, r1, rb1), (g2, r2, rb2))):
        gather_end(i, g)
        coef_end(i, r, rb)
        for j in range(CHUNKS):
            partial_send(i, j).wait_send()
    for step in range(1, 8):
        share(step).wait_send()


def shards(orbitals, potential, rot_first, rot_second):
    bf16, f32 = jnp.bfloat16, jnp.float32
    vmem = pl.BlockSpec(memory_space=pltpu.VMEM)
    dma = pltpu.SemaphoreType.DMA
    result = pl.pallas_call(
        kernel,
        out_shape=jax.ShapeDtypeStruct((ROWS, LANES), bf16),
        in_specs=[vmem] * 4,
        out_specs=vmem,
        scratch_shapes=[
            pltpu.VMEM((EXT * NY, HALF), bf16),
            pltpu.VMEM((EXT * NY, HALF), bf16),
            pltpu.VMEM((EXT, NY + 16, HALF), f32),
            pltpu.VMEM((GRID_X, NY), f32),
            pltpu.VMEM((PAIR, NY, HALF), f32),
            pltpu.VMEM((PAIR * NY, HALF), bf16),
            pltpu.VMEM((16, ROWS, LANES), bf16),
            pltpu.VMEM((16, ROWS, LANES), bf16),
            pltpu.VMEM((2, 4096, LANES), bf16),
            pltpu.VMEM((2, 4096, LANES), bf16),
            pltpu.VMEM((2, CHUNKS, CROWS, LANES), bf16),
            pltpu.VMEM((2, CHUNKS, CROWS, LANES), bf16),
            pltpu.VMEM((CHUNKS, CROWS, LANES), f32),
            pltpu.VMEM((8, 8, LANES), f32),
            dma, dma,
            dma((CHUNKS,)), dma((CHUNKS,)),
            dma((1 + CHUNKS,)),
            dma((2, 2)), dma((2, 2)),
            dma((2, CHUNKS, 17)), dma((2, CHUNKS, 16)),
            dma((2, CHUNKS)), dma((2, CHUNKS)),
            dma((7,)), dma((7,)),
            dma((2, PIECES, 2)), dma((2, PIECES, 2)),
            dma((2, 2, PIECES, 4)), dma((2, 2, PIECES, 4)),
        ],
        compiler_params=pltpu.CompilerParams(
            collective_id=0, has_side_effects=True, vmem_limit_bytes=56 << 20
        ),
    )(orbitals.reshape(ROWS, LANES), potential, rot_first, rot_second)
    return result.reshape(OWN, NY, LANES)


def solution(mesh):
    placed = (P("dom", None, "band"), P(), P("dom", "band"), P("dom", "band"))
    return jax.shard_map(
        shards, mesh=mesh, in_specs=placed, out_specs=P("dom", None, "band"), check_vma=False
    )
```

```python
import functools

import jax
import jax.numpy as jnp
from jax import lax
from jax.experimental import pallas as pl
from jax.experimental.pallas import tpu as pltpu
from jax.sharding import PartitionSpec as P

stencil_weights = (
    -5369.0 / 1800.0,
    12.0 / 7.0,
    -15.0 / 56.0,
    10.0 / 189.0,
    -1.0 / 112.0,
    2.0 / 1925.0,
    -1.0 / 16632.0,
)
filter_center = 3.8
filter_half = 3.3

MESH = pl.DeviceIdType.MESH
GRID_X = 96
NY = 64
OWN = 12
ROWS = OWN * NY
LANES = 256
HALF = 128
CHUNKS = 3
CROWS = ROWS // CHUNKS
PAIR = 2 * OWN
EXT = PAIR + 12
CELLS = GRID_X * NY
PIECES = 4
PROWS = 1024 // PIECES


def aligned(value, multiple):
    return pl.multiple_of(value, multiple)


def kernel(
    orb, pot, r1, r2, out,
    oext, dext, vpad, potf, volt, filt, g1, g2, rb1, rb2, relay, pbuf, prec, tq, sq,
    swap_s, swap_r, back_s, back_r, loc, halo_s, halo_r,
    g_s, g_r, p_s, p_r, sq_s, sq_r, rz_s, rz_r, rl_r, ry_s, ry_r,
):
    band = lax.axis_index("band")
    dom = lax.axis_index("dom")
    x = band // 8
    zl = (band // 2) % 4
    za = zl // 2
    zb = zl % 2
    core = band % 2
    y = dom // 2
    zh = dom % 2

    def device(x_=None, y_=None, zh_=None, za_=None, zb_=None, core_=None):
        pick = lambda new, old: old if new is None else new
        b = pick(x_, x) * 8 + (pick(za_, za) * 2 + pick(zb_, zb)) * 2 + pick(core_, core)
        d = pick(y_, y) * 2 + pick(zh_, zh)
        return {"band": b, "dom": d}

    def around(value, step):
        return (value + step) % 4

    def remote(src, dst, send, recv, to):
        return pltpu.make_async_remote_copy(
            src_ref=src, dst_ref=dst, send_sem=send, recv_sem=recv, device_id=to, device_id_type=MESH
        )

    barrier = pltpu.get_barrier_semaphore()
    partners = []
    for step in range(1, 8):
        z = (zh * 4 + zl + step) % 8
        partners.append(device(zh_=z // 4, za_=(z // 2) % 2, zb_=z % 2))
    for step in range(1, 4):
        partners.append(device(x_=around(x, step)))
        partners.append(device(y_=around(y, step)))
        partners.append(device(y_=around(y, step), zh_=1 - zh))
    partners.append(device(core_=1 - core))
    for to in partners:
        pl.semaphore_signal(barrier, inc=1, device_id=to, device_id_type=MESH)
    pl.semaphore_wait(barrier, len(partners))

    mine = aligned(zh * HALF, HALF)
    theirs = aligned((1 - zh) * HALF, HALF)
    own_at = aligned((6 + OWN * zh) * NY, NY)
    partner_at = aligned((6 + OWN * (1 - zh)) * NY, NY)
    swap = remote(
        orb.at[:, pl.ds(theirs, HALF)], oext.at[pl.ds(own_at, ROWS)], swap_s, swap_r, device(zh_=1 - zh)
    )
    swap.start()
    keep = pltpu.make_async_copy(orb.at[:, pl.ds(mine, HALF)], oext.at[pl.ds(own_at, ROWS)], loc.at[0])
    keep.start()

    def piece(q):
        return pl.ds(q * PROWS, PROWS)

    def slot_rows(step, q, first=0, count=PROWS):
        return pl.ds(aligned(around(y, step) * 1024 + q * PROWS + first, 128), count)

    def coef_z(i, r, rb, q):
        here = rb.at[za, slot_rows(0, q)]
        other = remote(r.at[piece(q)], here, rz_s.at[i, q, 0], rz_r.at[i, q, za], device(zh_=1 - zh, za_=zh))
        near = remote(r.at[piece(q)], here, rz_s.at[i, q, 1], rz_r.at[i, q, za], device(za_=zh))
        over = remote(
            r.at[piece(q)], relay.at[i, piece(q)], rz_s.at[i, q, 0], rl_r.at[i, q], device(zh_=1 - zh, za_=1 - za)
        )
        onward = remote(
            relay.at[i, piece(q)], rb.at[1 - za, slot_rows(0, q)], rz_s.at[i, q, 1], rz_r.at[i, q, 1 - za],
            device(za_=1 - za),
        )
        own = pltpu.make_async_copy(r.at[piece(q)], here, rz_r.at[i, q, za])
        return other, near, over, onward, own

    def coef_z_start(i, r, rb, q):
        other, near, over, onward, own = coef_z(i, r, rb, q)

        @pl.when(za != zh)
        def _():
            other.start()
            near.start()

        @pl.when(za == zh)
        def _():
            over.start()
            own.start()

    def coef_onward(i, r, rb, q):
        other, near, over, onward, own = coef_z(i, r, rb, q)

        @pl.when(za == zh)
        def _():
            over.wait_recv()
            onward.start()

    def ring(i, rb, part, q, n, step, to, first=0, count=PROWS):
        rows = slot_rows(step, q, first, count)
        return remote(
            rb.at[part, rows], rb.at[part, rows], ry_s.at[i, part, q, n], ry_r.at[i, part, q, n],
            device(y_=around(y, to)),
        )

    def coef_near(i, rb, q):
        return [ring(i, rb, part, q, n, 0, to) for part in range(2) for n, to in ((0, 1), (1, 3))]

    def coef_far(i, rb, q):
        half = PROWS // 2
        return [
            ring(i, rb, part, q, n, step, to, first, half)
            for part in range(2)
            for n, step, to, first in ((2, 3, 1, 0), (3, 1, 3, half))
        ]

    def coef_near_start(i, r, rb, q):
        for part in range(2):
            pltpu.make_async_copy(r.at[piece(q)], rb.at[part, slot_rows(0, q)], rz_r.at[i, q, part]).wait()
        for copy in coef_near(i, rb, q):
            copy.start()

    def coef_far_start(i, rb, q):
        for copy in coef_near(i, rb, q):
            copy.wait_recv()
        for copy in coef_far(i, rb, q):
            copy.start()

    def coef_wait(i, rb):
        for q in range(PIECES):
            for copy in coef_far(i, rb, q):
                copy.wait_recv()

    def coef_end(i, r, rb):
        for q in range(PIECES):
            other, near, over, onward, own = coef_z(i, r, rb, q)

            @pl.when(za != zh)
            def _():
                other.wait_send()
                near.wait_send()

            @pl.when(za == zh)
            def _():
                over.wait_send()
                onward.wait_send()

            for copy in coef_near(i, rb, q) + coef_far(i, rb, q):
                copy.wait_send()

    coef_z_start(0, r1, rb1, 0)

    diagonal = lax.broadcasted_iota(jnp.int32, (NY, NY), 0) == lax.broadcasted_iota(jnp.int32, (NY, NY), 1)
    ones = jnp.ones((NY, HALF), jnp.bfloat16)

    potf[...] = pot[...].astype(jnp.float32)

    def spread(i, carry):
        row = potf[pl.ds(y * PAIR + i, 1), :]
        square = jnp.where(diagonal, jnp.broadcast_to(row, (NY, NY)), 0.0).astype(jnp.bfloat16)
        volt[i] = jnp.dot(square, ones, preferred_element_type=jnp.float32)
        return carry

    lax.fori_loop(0, PAIR, spread, 0)

    def clear(i, carry):
        vpad[i, 0:8, :] = jnp.zeros((8, HALF), jnp.float32)
        vpad[i, 72:80, :] = jnp.zeros((8, HALF), jnp.float32)
        return carry

    lax.fori_loop(0, EXT, clear, 0)

    def rims(i, ext):
        up = remote(
            ext.at[pl.ds(24 * NY, 6 * NY)], ext.at[pl.ds(0, 6 * NY)], halo_s.at[i, 0], halo_r.at[i, 0],
            device(y_=around(y, 1)),
        )
        down = remote(
            ext.at[pl.ds(6 * NY, 6 * NY)], ext.at[pl.ds(30 * NY, 6 * NY)], halo_s.at[i, 1], halo_r.at[i, 1],
            device(y_=around(y, 3)),
        )
        return up, down

    def widen(ext, first, count, keep_it):
        def step(i, carry):
            at = first + i
            value = ext[pl.ds(aligned(at * NY, NY), NY), :].astype(jnp.float32)
            if keep_it is not None:
                value = jnp.where(keep_it, value, 0.0)
            vpad[at, 8:72, :] = value
            return carry

        lax.fori_loop(0, count, step, 0)

    def applied(i):
        center = vpad[i + 6, 8:72, :]
        lap = 2.0 * stencil_weights[0] * center
        for k in range(1, 7):
            lap = lap + stencil_weights[k] * (
                (vpad[i + 6 + k, 8:72, :] + vpad[i + 6 - k, 8:72, :])
                + (vpad[i + 6, 8 + k : 72 + k, :] + vpad[i + 6, 8 - k : 72 - k, :])
            )
        return -0.5 * lap + volt[i] * center, center

    coef_z_start(0, r1, rb1, 1)
    coef_onward(0, r1, rb1, 0)
    keep.wait()
    swap.wait_recv()
    for copy in rims(0, oext):
        copy.start()
    coef_z_start(0, r1, rb1, 2)
    coef_z_start(0, r1, rb1, 3)
    coef_near_start(0, r1, rb1, 0)
    widen(oext, 6, PAIR, None)
    for copy in rims(0, oext):
        copy.wait_recv()
    widen(oext, 0, 6, y > 0)
    widen(oext, 30, 6, y < 3)
    coef_onward(0, r1, rb1, 1)

    def first(i, carry):
        value, center = applied(i)
        dext[pl.ds(aligned((i + 6) * NY, NY), NY), :] = (
            (value - filter_center * center) * (1.0 / filter_half)
        ).astype(jnp.bfloat16)
        return carry

    lax.fori_loop(0, PAIR, first, 0)
    for copy in rims(1, dext):
        copy.start()
    coef_near_start(0, r1, rb1, 1)
    widen(dext, 6, PAIR, None)
    for copy in rims(1, dext):
        copy.wait_recv()
    widen(dext, 0, 6, y > 0)
    widen(dext, 30, 6, y < 3)
    coef_onward(0, r1, rb1, 2)

    def second(i, carry):
        value, center = applied(i)
        start = oext[pl.ds(aligned((i + 6) * NY, NY), NY), :].astype(jnp.float32)
        filt[pl.ds(aligned(i * NY, NY), NY), :] = (
            (value - filter_center * center) * (2.0 / filter_half) - start
        ).astype(jnp.bfloat16)
        return carry

    own_slot = (x * 2 + zb) * 2 + core
    half_lanes = pl.ds(mine, HALF)

    def back(j):
        source = filt.at[pl.ds(aligned((1 - zh) * ROWS + j * CROWS, CROWS), CROWS)]
        place = g1.at[own_slot, pl.ds(j * CROWS, CROWS), half_lanes]
        return remote(source, place, back_s.at[j], back_r.at[j], device(zh_=1 - zh))

    def stay(j):
        source = filt.at[pl.ds(aligned(zh * ROWS + j * CROWS, CROWS), CROWS)]
        place = g1.at[own_slot, pl.ds(j * CROWS, CROWS), half_lanes]
        return pltpu.make_async_copy(source, place, loc.at[1 + j])

    per = OWN // CHUNKS
    for j in range(CHUNKS):
        lax.fori_loop((1 - zh) * OWN + j * per, (1 - zh) * OWN + (j + 1) * per, second, 0)
        back(j).start()
    coef_far_start(0, rb1, 0)
    coef_near_start(0, r1, rb1, 2)
    coef_onward(0, r1, rb1, 3)
    for j in range(CHUNKS):
        lax.fori_loop(zh * OWN + j * per, zh * OWN + (j + 1) * per, second, 0)
        stay(j).start()

    other_core = device(core_=1 - core)

    def block(g, slot, j):
        return g.at[slot, pl.ds(aligned(j * CROWS, CROWS), CROWS)]

    def send(i, g, slot, j, n, to):
        return remote(block(g, slot, j), block(g, slot, j), g_s.at[i, j, n], g_r.at[i, j, slot], to)

    right, left = device(x_=around(x, 1)), device(x_=around(x, 3))

    def slot_at(step, b):
        return (around(x, step) * 2 + b) * 2 + core

    def own_sends(i, g, j):
        return [send(i, g, own_slot, j, n, to) for n, to in enumerate((device(zb_=1 - zb), right, left, other_core))]

    def pair_sends(i, g, j):
        return [send(i, g, slot_at(0, 1 - zb), j, 4 + n, to) for n, to in enumerate((right, left, other_core))]

    def near_sends(i, g, j):
        sends = []
        for step, first, to in ((3, 0, right), (1, CROWS // 2, left)):
            for b in (0, 1):
                slot = slot_at(step, b)
                rows = pl.ds(aligned(j * CROWS + first, CROWS // 2), CROWS // 2)
                part = g.at[slot, rows]
                n = 7 + len(sends)
                sends.append(remote(part, part, g_s.at[i, j, n], g_r.at[i, j, slot], to))
                sends.append(send(i, g, slot, j, n + 1, other_core))
        return sends

    def far_sends(i, g, j):
        return [send(i, g, slot_at(2, b), j, 15 + b, other_core) for b in (0, 1)]

    def arrived(i, g, slot, j):
        send(i, g, slot, j, 0, other_core).wait_recv()

    def gather_own(i, g, j):
        for copy in own_sends(i, g, j):
            copy.start()

    def gather_pair(i, g, j):
        arrived(i, g, slot_at(0, 1 - zb), j)
        for copy in pair_sends(i, g, j):
            copy.start()

    def gather_near(i, g, j):
        for step in (3, 1):
            for b in (0, 1):
                arrived(i, g, slot_at(step, b), j)
        for copy in near_sends(i, g, j):
            copy.start()

    def gather_far(i, g, j):
        for b in (0, 1):
            arrived(i, g, slot_at(2, b), j)
        for copy in far_sends(i, g, j):
            copy.start()
        for slot in range(8):
            arrived(i, g, slot * 2 + 1 - core, j)

    def gather_end(i, g):
        def step(j, carry):
            for copy in own_sends(i, g, j) + pair_sends(i, g, j) + near_sends(i, g, j) + far_sends(i, g, j):
                copy.wait_send()
            return carry

        lax.fori_loop(0, CHUNKS, step, 0)

    def product(g, rb, j, part):
        rows = pl.ds(aligned(j * CROWS, CROWS), CROWS)
        total = None
        for slot in range(16):
            term = jnp.dot(
                g[slot, rows, :], rb[part, slot * LANES : (slot + 1) * LANES, :], preferred_element_type=jnp.float32
            )
            total = term if total is None else total + term
        return total

    def partial_send(i, j):
        return remote(pbuf.at[i, j], prec.at[i, j], p_s.at[i, j], p_r.at[i, j], device(za_=1 - za))

    def multiply(i, g, rb, j):
        gather_far(i, g, j)
        pbuf[i, j] = product(g, rb, j, 1 - za).astype(jnp.bfloat16)
        partial_send(i, j).start()
        tq[j] = product(g, rb, j, za)

    for j in range(CHUNKS):
        stay(j).wait()
        back(j).wait_recv()
        gather_own(0, g1, j)
    coef_near_start(0, r1, rb1, 3)
    coef_far_start(0, rb1, 1)
    for j in range(CHUNKS):
        gather_pair(0, g1, j)
    coef_far_start(0, rb1, 2)
    for q in range(PIECES):
        coef_z_start(1, r2, rb2, q)
    gather_near(0, g1, 0)
    gather_near(0, g1, 1)
    coef_far_start(0, rb1, 3)
    coef_wait(0, rb1)
    multiply(0, g1, rb1, 0)
    coef_onward(1, r2, rb2, 0)
    gather_near(0, g1, 2)
    coef_onward(1, r2, rb2, 1)
    multiply(0, g1, rb1, 1)
    coef_onward(1, r2, rb2, 2)
    coef_near_start(1, r2, rb2, 0)
    multiply(0, g1, rb1, 2)
    coef_near_start(1, r2, rb2, 1)
    coef_onward(1, r2, rb2, 3)

    sums = jnp.zeros((8, LANES), jnp.float32)
    for j in range(CHUNKS):
        partial_send(0, j).wait_recv()

        def squares(n, total):
            rows = pl.ds(aligned(n * 32, 32), 32)
            value = tq[j, rows, :] + prec[0, j, rows, :].astype(jnp.float32)
            tq[j, rows, :] = value
            return total + jnp.sum((value * value).reshape(4, 8, LANES), axis=0)

        sums = lax.fori_loop(0, CROWS // 32, squares, sums)
    sq[dom] = sums

    def share(step):
        to = (dom + step) % 8
        return remote(sq.at[dom], sq.at[dom], sq_s.at[step - 1], sq_r.at[step - 1], {"band": band, "dom": to})

    for step in range(1, 8):
        share(step).start()
    for step in range(1, 8):
        share(step).wait_recv()
    total = sq[0]
    for d in range(1, 8):
        total = total + sq[d]
    mean_square = jnp.sum(total, axis=0, keepdims=True) * (1.0 / CELLS)
    scale = 1.0 / jnp.sqrt(mean_square + 1e-06)
    for j in range(CHUNKS):

        def normalize(n, carry):
            rows = pl.ds(aligned(n * 32, 32), 32)
            g2[own_slot, pl.ds(aligned(j * CROWS + n * 32, 32), 32), :] = (tq[j, rows, :] * scale).astype(jnp.bfloat16)
            return carry

        lax.fori_loop(0, CROWS // 32, normalize, 0)
        gather_own(1, g2, j)

    coef_near_start(1, r2, rb2, 2)
    coef_far_start(1, rb2, 0)
    coef_near_start(1, r2, rb2, 3)
    coef_far_start(1, rb2, 1)
    for j in range(CHUNKS):
        gather_pair(1, g2, j)
    coef_far_start(1, rb2, 2)
    gather_near(1, g2, 0)
    gather_near(1, g2, 1)
    coef_far_start(1, rb2, 3)
    coef_wait(1, rb2)
    multiply(1, g2, rb2, 0)
    gather_near(1, g2, 2)
    multiply(1, g2, rb2, 1)
    multiply(1, g2, rb2, 2)

    for j in range(CHUNKS):
        partial_send(1, j).wait_recv()

        def finish(n, carry):
            rows = pl.ds(aligned(n * 32, 32), 32)
            out[pl.ds(aligned(j * CROWS + n * 32, 32), 32), :] = (
                tq[j, rows, :] + prec[1, j, rows, :].astype(jnp.float32)
            ).astype(jnp.bfloat16)
            return carry

        lax.fori_loop(0, CROWS // 32, finish, 0)

    swap.wait_send()
    for j in range(CHUNKS):
        back(j).wait_send()
    for i, ext in ((0, oext), (1, dext)):
        for copy in rims(i, ext):
            copy.wait_send()
    for i, (g, r, rb) in enumerate(((g1, r1, rb1), (g2, r2, rb2))):
        gather_end(i, g)
        coef_end(i, r, rb)
        for j in range(CHUNKS):
            partial_send(i, j).wait_send()
    for step in range(1, 8):
        share(step).wait_send()


def shards(orbitals, potential, rot_first, rot_second):
    bf16, f32 = jnp.bfloat16, jnp.float32
    vmem = pl.BlockSpec(memory_space=pltpu.VMEM)
    dma = pltpu.SemaphoreType.DMA
    result = pl.pallas_call(
        kernel,
        out_shape=jax.ShapeDtypeStruct((ROWS, LANES), bf16),
        in_specs=[vmem] * 4,
        out_specs=vmem,
        scratch_shapes=[
            pltpu.VMEM((EXT * NY, HALF), bf16),
            pltpu.VMEM((EXT * NY, HALF), bf16),
            pltpu.VMEM((EXT, NY + 16, HALF), f32),
            pltpu.VMEM((GRID_X, NY), f32),
            pltpu.VMEM((PAIR, NY, HALF), f32),
            pltpu.VMEM((PAIR * NY, HALF), bf16),
            pltpu.VMEM((16, ROWS, LANES), bf16),
            pltpu.VMEM((16, ROWS, LANES), bf16),
            pltpu.VMEM((2, 4096, LANES), bf16),
            pltpu.VMEM((2, 4096, LANES), bf16),
            pltpu.VMEM((2, 1024, LANES), bf16),
            pltpu.VMEM((2, CHUNKS, CROWS, LANES), bf16),
            pltpu.VMEM((2, CHUNKS, CROWS, LANES), bf16),
            pltpu.VMEM((CHUNKS, CROWS, LANES), f32),
            pltpu.VMEM((8, 8, LANES), f32),
            dma, dma,
            dma((CHUNKS,)), dma((CHUNKS,)),
            dma((1 + CHUNKS,)),
            dma((2, 2)), dma((2, 2)),
            dma((2, CHUNKS, 17)), dma((2, CHUNKS, 16)),
            dma((2, CHUNKS)), dma((2, CHUNKS)),
            dma((7,)), dma((7,)),
            dma((2, PIECES, 2)), dma((2, PIECES, 2)), dma((2, PIECES)),
            dma((2, 2, PIECES, 4)), dma((2, 2, PIECES, 4)),
        ],
        compiler_params=pltpu.CompilerParams(
            collective_id=0, has_side_effects=True, vmem_limit_bytes=56 << 20
        ),
    )(orbitals.reshape(ROWS, LANES), potential, rot_first, rot_second)
    return result.reshape(OWN, NY, LANES)


def solution(mesh):
    placed = (P("dom", None, "band"), P(), P("dom", "band"), P("dom", "band"))
    return jax.shard_map(
        shards, mesh=mesh, in_specs=placed, out_specs=P("dom", None, "band"), check_vma=False
    )
```

```python
import functools

import jax
import jax.numpy as jnp
from jax import lax
from jax.experimental import pallas as pl
from jax.experimental.pallas import tpu as pltpu
from jax.sharding import PartitionSpec as P

stencil_weights = (
    -5369.0 / 1800.0,
    12.0 / 7.0,
    -15.0 / 56.0,
    10.0 / 189.0,
    -1.0 / 112.0,
    2.0 / 1925.0,
    -1.0 / 16632.0,
)
filter_center = 3.8
filter_half = 3.3

MESH = pl.DeviceIdType.MESH
GRID_X = 96
NY = 64
OWN = 12
ROWS = OWN * NY
LANES = 256
HALF = 128
CHUNKS = 3
CROWS = ROWS // CHUNKS
PAIR = 2 * OWN
EXT = PAIR + 12
CELLS = GRID_X * NY
PIECES = 2
PROWS = 1024 // PIECES


SCHEDULE = {
    "swap": "z00",
    "rim0": "z01",
    "first": "o00",
    "back": "o01",
    "stay": "n00",
    "own00": "n01",
    "own02": "z10 f00",
    "pair00": "z11",
    "near00": "f01",
    "near01": "o10 o11",
    "mul00": "n10 n11",
    "turn2": "f10",
    "norm": "f11",
}


def aligned(value, multiple):
    return pl.multiple_of(value, multiple)


def kernel(
    orb, pot, r1, r2, out,
    oext, dext, vpad, potf, volt, filt, g1, g2, rb1, rb2, relay, pbuf, prec, tq, sq, norm, lhs,
    swap_s, swap_r, back_s, back_r, loc, halo_s, halo_r,
    g_s, g_r, p_s, p_r, sq_s, sq_r, n_s, n_r, rz_s, rz_r, rl_r, ry_s, ry_r,
):
    band = lax.axis_index("band")
    dom = lax.axis_index("dom")
    x = band // 8
    zl = (band // 2) % 4
    za = zl // 2
    zb = zl % 2
    core = band % 2
    y = dom // 2
    zh = dom % 2

    def device(x_=None, y_=None, zh_=None, za_=None, zb_=None, core_=None):
        pick = lambda new, old: old if new is None else new
        b = pick(x_, x) * 8 + (pick(za_, za) * 2 + pick(zb_, zb)) * 2 + pick(core_, core)
        d = pick(y_, y) * 2 + pick(zh_, zh)
        return {"band": b, "dom": d}

    def around(value, step):
        return (value + step) % 4

    def remote(src, dst, send, recv, to):
        return pltpu.make_async_remote_copy(
            src_ref=src, dst_ref=dst, send_sem=send, recv_sem=recv, device_id=to, device_id_type=MESH
        )

    barrier = pltpu.get_barrier_semaphore()
    partners = []
    for step in range(1, 8):
        z = (zh * 4 + zl + step) % 8
        partners.append(device(zh_=z // 4, za_=(z // 2) % 2, zb_=z % 2))
    for step in range(1, 4):
        partners.append(device(x_=around(x, step)))
        partners.append(device(y_=around(y, step)))
        partners.append(device(y_=around(y, step), zh_=1 - zh))
        partners.append(device(x_=around(x, step), zb_=1 - zb))
    partners.append(device(core_=1 - core))
    for to in partners:
        pl.semaphore_signal(barrier, inc=1, device_id=to, device_id_type=MESH)
    pl.semaphore_wait(barrier, len(partners))

    mine = aligned(zh * HALF, HALF)
    theirs = aligned((1 - zh) * HALF, HALF)
    own_at = aligned((6 + OWN * zh) * NY, NY)
    partner_at = aligned((6 + OWN * (1 - zh)) * NY, NY)
    swap = remote(
        orb.at[:, pl.ds(theirs, HALF)], oext.at[pl.ds(own_at, ROWS)], swap_s, swap_r, device(zh_=1 - zh)
    )
    swap.start()
    keep = pltpu.make_async_copy(orb.at[:, pl.ds(mine, HALF)], oext.at[pl.ds(own_at, ROWS)], loc.at[0])
    keep.start()

    def piece(q):
        return pl.ds(q * PROWS, PROWS)

    def slot_rows(step, q, first=0, count=PROWS):
        return pl.ds(aligned(around(y, step) * 1024 + q * PROWS + first, 128), count)

    def coef_z(i, r, rb, q):
        here = rb.at[za, slot_rows(0, q)]
        other = remote(r.at[piece(q)], here, rz_s.at[i, q, 0], rz_r.at[i, q, za], device(zh_=1 - zh, za_=zh))
        near = remote(r.at[piece(q)], here, rz_s.at[i, q, 1], rz_r.at[i, q, za], device(za_=zh))
        over = remote(
            r.at[piece(q)], relay.at[i, piece(q)], rz_s.at[i, q, 0], rl_r.at[i, q], device(zh_=1 - zh, za_=1 - za)
        )
        onward = remote(
            relay.at[i, piece(q)], rb.at[1 - za, slot_rows(0, q)], rz_s.at[i, q, 1], rz_r.at[i, q, 1 - za],
            device(za_=1 - za),
        )
        own = pltpu.make_async_copy(r.at[piece(q)], here, rz_r.at[i, q, za])
        return other, near, over, onward, own

    def coef_z_start(i, r, rb, q):
        other, near, over, onward, own = coef_z(i, r, rb, q)

        @pl.when(za != zh)
        def _():
            other.start()
            near.start()

        @pl.when(za == zh)
        def _():
            over.start()
            own.start()

    def coef_onward(i, r, rb, q):
        other, near, over, onward, own = coef_z(i, r, rb, q)

        @pl.when(za == zh)
        def _():
            over.wait_recv()
            onward.start()

    def ring(i, rb, part, q, n, step, to, first=0, count=PROWS):
        rows = slot_rows(step, q, first, count)
        return remote(
            rb.at[part, rows], rb.at[part, rows], ry_s.at[i, part, q, n], ry_r.at[i, part, q, n],
            device(y_=around(y, to)),
        )

    def coef_near(i, rb, q):
        return [ring(i, rb, part, q, n, 0, to) for part in range(2) for n, to in ((0, 1), (1, 3))]

    def coef_far(i, rb, q):
        half = PROWS // 2
        return [
            ring(i, rb, part, q, n, step, to, first, half)
            for part in range(2)
            for n, step, to, first in ((2, 3, 1, 0), (3, 1, 3, half))
        ]

    def coef_near_start(i, r, rb, q):
        for part in range(2):
            pltpu.make_async_copy(r.at[piece(q)], rb.at[part, slot_rows(0, q)], rz_r.at[i, q, part]).wait()
        for copy in coef_near(i, rb, q):
            copy.start()

    def coef_far_start(i, rb, q):
        for copy in coef_near(i, rb, q):
            copy.wait_recv()
        for copy in coef_far(i, rb, q):
            copy.start()

    def coef_wait(i, rb):
        for q in range(PIECES):
            for copy in coef_far(i, rb, q):
                copy.wait_recv()

    def coef_end(i, r, rb):
        for q in range(PIECES):
            other, near, over, onward, own = coef_z(i, r, rb, q)

            @pl.when(za != zh)
            def _():
                other.wait_send()
                near.wait_send()

            @pl.when(za == zh)
            def _():
                over.wait_send()
                onward.wait_send()

            for copy in coef_near(i, rb, q) + coef_far(i, rb, q):
                copy.wait_send()


    rotations = ((r1, rb1), (r2, rb2))

    def at(point):
        for word in SCHEDULE.get(point, "").split():
            i, q = int(word[1]), int(word[2])
            r, rb = rotations[i]
            if word[0] == "z":
                coef_z_start(i, r, rb, q)
            elif word[0] == "o":
                coef_onward(i, r, rb, q)
            elif word[0] == "n":
                coef_near_start(i, r, rb, q)
            else:
                coef_far_start(i, rb, q)

    at("start")

    diagonal = lax.broadcasted_iota(jnp.int32, (NY, NY), 0) == lax.broadcasted_iota(jnp.int32, (NY, NY), 1)
    ones = jnp.ones((NY, HALF), jnp.bfloat16)

    potf[...] = pot[...].astype(jnp.float32)

    def spread(i, carry):
        row = potf[pl.ds(y * PAIR + i, 1), :]
        square = jnp.where(diagonal, jnp.broadcast_to(row, (NY, NY)), 0.0).astype(jnp.bfloat16)
        volt[i] = jnp.dot(square, ones, preferred_element_type=jnp.float32)
        return carry

    lax.fori_loop(0, PAIR, spread, 0)

    def clear(i, carry):
        vpad[i, 0:8, :] = jnp.zeros((8, HALF), jnp.float32)
        vpad[i, 72:80, :] = jnp.zeros((8, HALF), jnp.float32)
        return carry

    lax.fori_loop(0, EXT, clear, 0)

    def rims(i, ext):
        up = remote(
            ext.at[pl.ds(24 * NY, 6 * NY)], ext.at[pl.ds(0, 6 * NY)], halo_s.at[i, 0], halo_r.at[i, 0],
            device(y_=around(y, 1)),
        )
        down = remote(
            ext.at[pl.ds(6 * NY, 6 * NY)], ext.at[pl.ds(30 * NY, 6 * NY)], halo_s.at[i, 1], halo_r.at[i, 1],
            device(y_=around(y, 3)),
        )
        return up, down

    def widen(ext, first, count, keep_it):
        def step(i, carry):
            at = first + i
            value = ext[pl.ds(aligned(at * NY, NY), NY), :].astype(jnp.float32)
            if keep_it is not None:
                value = jnp.where(keep_it, value, 0.0)
            vpad[at, 8:72, :] = value
            return carry

        lax.fori_loop(0, count, step, 0)

    def applied(i):
        center = vpad[i + 6, 8:72, :]
        lap = 2.0 * stencil_weights[0] * center
        for k in range(1, 7):
            lap = lap + stencil_weights[k] * (
                (vpad[i + 6 + k, 8:72, :] + vpad[i + 6 - k, 8:72, :])
                + (vpad[i + 6, 8 + k : 72 + k, :] + vpad[i + 6, 8 - k : 72 - k, :])
            )
        return -0.5 * lap + volt[i] * center, center

    at("volt")
    keep.wait()
    swap.wait_recv()
    for copy in rims(0, oext):
        copy.start()
    at("swap")
    widen(oext, 6, PAIR, None)
    for copy in rims(0, oext):
        copy.wait_recv()
    widen(oext, 0, 6, y > 0)
    widen(oext, 30, 6, y < 3)
    at("rim0")

    def first(i, carry):
        value, center = applied(i)
        dext[pl.ds(aligned((i + 6) * NY, NY), NY), :] = (
            (value - filter_center * center) * (1.0 / filter_half)
        ).astype(jnp.bfloat16)
        return carry

    lax.fori_loop(0, PAIR, first, 0)
    for copy in rims(1, dext):
        copy.start()
    at("first")
    widen(dext, 6, PAIR, None)
    for copy in rims(1, dext):
        copy.wait_recv()
    widen(dext, 0, 6, y > 0)
    widen(dext, 30, 6, y < 3)
    at("rim1")

    def second(i, carry):
        value, center = applied(i)
        start = oext[pl.ds(aligned((i + 6) * NY, NY), NY), :].astype(jnp.float32)
        filt[pl.ds(aligned(i * NY, NY), NY), :] = (
            (value - filter_center * center) * (2.0 / filter_half) - start
        ).astype(jnp.bfloat16)
        return carry

    own_slot = (x * 2 + zb) * 2 + core
    half_lanes = pl.ds(mine, HALF)

    def back(j):
        source = filt.at[pl.ds(aligned((1 - zh) * ROWS + j * CROWS, CROWS), CROWS)]
        place = g1.at[own_slot, pl.ds(j * CROWS, CROWS), half_lanes]
        return remote(source, place, back_s.at[j], back_r.at[j], device(zh_=1 - zh))

    def stay(j):
        source = filt.at[pl.ds(aligned(zh * ROWS + j * CROWS, CROWS), CROWS)]
        place = g1.at[own_slot, pl.ds(j * CROWS, CROWS), half_lanes]
        return pltpu.make_async_copy(source, place, loc.at[1 + j])

    per = OWN // CHUNKS
    for j in range(CHUNKS):
        lax.fori_loop((1 - zh) * OWN + j * per, (1 - zh) * OWN + (j + 1) * per, second, 0)
        back(j).start()
    at("back")
    for j in range(CHUNKS):
        lax.fori_loop(zh * OWN + j * per, zh * OWN + (j + 1) * per, second, 0)
        stay(j).start()

    other_core = device(core_=1 - core)

    def block(g, slot, j):
        return g.at[slot, pl.ds(aligned(j * CROWS, CROWS), CROWS)]

    def send(i, g, slot, j, n, to):
        return remote(block(g, slot, j), block(g, slot, j), g_s.at[i, j, n], g_r.at[i, j, slot], to)

    right, left = device(x_=around(x, 1)), device(x_=around(x, 3))

    def slot_at(step, b):
        return (around(x, step) * 2 + b) * 2 + core

    def own_sends(i, g, j):
        return [send(i, g, own_slot, j, n, to) for n, to in enumerate((device(zb_=1 - zb), right, left, other_core))]

    def pair_sends(i, g, j):
        return [send(i, g, slot_at(0, 1 - zb), j, 4 + n, to) for n, to in enumerate((right, left, other_core))]

    def near_sends(i, g, j):
        sends = []
        for step, first, to in ((3, 0, right), (1, CROWS // 2, left)):
            for b in (0, 1):
                slot = slot_at(step, b)
                rows = pl.ds(aligned(j * CROWS + first, CROWS // 2), CROWS // 2)
                part = g.at[slot, rows]
                n = 7 + len(sends)
                sends.append(remote(part, part, g_s.at[i, j, n], g_r.at[i, j, slot], to))
                sends.append(send(i, g, slot, j, n + 1, other_core))
        return sends

    def far_sends(i, g, j):
        return [send(i, g, slot_at(2, b), j, 15 + b, other_core) for b in (0, 1)]

    def arrived(i, g, slot, j):
        send(i, g, slot, j, 0, other_core).wait_recv()

    def gather_own(i, g, j):
        for copy in own_sends(i, g, j):
            copy.start()

    def gather_pair(i, g, j):
        arrived(i, g, slot_at(0, 1 - zb), j)
        for copy in pair_sends(i, g, j):
            copy.start()

    def gather_near(i, g, j):
        for step in (3, 1):
            for b in (0, 1):
                arrived(i, g, slot_at(step, b), j)
        for copy in near_sends(i, g, j):
            copy.start()

    def gather_far(i, g, j):
        for b in (0, 1):
            arrived(i, g, slot_at(2, b), j)
        for copy in far_sends(i, g, j):
            copy.start()
        for slot in range(8):
            arrived(i, g, slot * 2 + 1 - core, j)

    def gather_end(i, g):
        def step(j, carry):
            for copy in own_sends(i, g, j) + pair_sends(i, g, j) + near_sends(i, g, j) + far_sends(i, g, j):
                copy.wait_send()
            return carry

        lax.fori_loop(0, CHUNKS, step, 0)

    def product(g, rb, j, part):
        rows = pl.ds(aligned(j * CROWS, CROWS), CROWS)
        total = None
        for slot in range(16):
            term = jnp.dot(
                g[slot, rows, :], rb[part, slot * LANES : (slot + 1) * LANES, :], preferred_element_type=jnp.float32
            )
            total = term if total is None else total + term
        return total

    def partial_send(i, j):
        return remote(pbuf.at[i, j], prec.at[i, j], p_s.at[i, j], p_r.at[i, j], device(za_=1 - za))

    def multiply(i, g, rb, j):
        gather_far(i, g, j)
        pbuf[i, j] = product(g, rb, j, 1 - za).astype(jnp.bfloat16)
        partial_send(i, j).start()
        tq[j] = product(g, rb, j, za)

    at("stay")
    for j in range(CHUNKS):
        stay(j).wait()
        back(j).wait_recv()
        gather_own(0, g1, j)
        at(f"own0{j}")
    for j in range(CHUNKS):
        gather_pair(0, g1, j)
        at(f"pair0{j}")
    gather_near(0, g1, 0)
    at("near00")
    gather_near(0, g1, 1)
    at("near01")
    coef_wait(0, rb1)
    multiply(0, g1, rb1, 0)
    at("mul00")
    gather_near(0, g1, 2)
    at("near02")
    multiply(0, g1, rb1, 1)
    at("mul01")

    def turned(j, sums):
        partial_send(0, j).wait_recv()

        def step(n, total):
            rows = pl.ds(aligned(n * 32, 32), 32)
            value = tq[j, rows, :] + prec[0, j, rows, :].astype(jnp.float32)
            g2[own_slot, pl.ds(aligned(j * CROWS + n * 32, 32), 32), :] = value.astype(jnp.bfloat16)
            return total + jnp.sum((value * value).reshape(4, 8, LANES), axis=0)

        sums = lax.fori_loop(0, CROWS // 32, step, sums)
        gather_own(1, g2, j)
        return sums

    sums = turned(0, jnp.zeros((8, LANES), jnp.float32))
    at("turn0")
    multiply(0, g1, rb1, 2)
    at("mul02")
    sums = turned(1, sums)
    at("turn1")
    gather_pair(1, g2, 0)
    at("pair10")
    sums = turned(2, sums)
    at("turn2")
    sq[dom] = sums

    def share(step):
        to = (dom + step) % 8
        return remote(sq.at[dom], sq.at[dom], sq_s.at[step - 1], sq_r.at[step - 1], {"band": band, "dom": to})

    for step in range(1, 8):
        share(step).start()
    for step in range(1, 8):
        share(step).wait_recv()
    total = sq[0]
    for d in range(1, 8):
        total = total + sq[d]
    mean_square = jnp.sum(total, axis=0, keepdims=True) * (1.0 / CELLS)
    norm[own_slot] = jnp.broadcast_to(1.0 / jnp.sqrt(mean_square + 1e-06), (8, LANES))

    def norm_send(slot, n, to):
        return remote(norm.at[slot], norm.at[slot], n_s.at[n], n_r.at[slot], to)

    others = [(step, b) for step in range(4) for b in (0, 1) if step or b]

    def norm_sends():
        sends = [norm_send(own_slot, 0, other_core)]
        for n, (step, b) in enumerate(others):
            sends.append(norm_send(own_slot, 1 + n, device(x_=around(x, step), zb_=(zb + b) % 2)))
        return sends

    def norm_forwards():
        return [
            norm_send(slot_at(step, (zb + b) % 2), 8 + n, other_core) for n, (step, b) in enumerate(others)
        ]

    for copy in norm_sends():
        copy.start()
    at("norm")
    gather_pair(1, g2, 1)
    at("pair11")
    gather_near(1, g2, 0)
    at("near10")
    gather_pair(1, g2, 2)
    at("pair12")
    for copy in norm_forwards():
        copy.wait_recv()
        copy.start()
    gather_near(1, g2, 1)
    at("near11")
    for slot in range(8):
        norm_send(slot * 2 + 1 - core, 0, other_core).wait_recv()

    def normalize(j):
        def step(slot, carry):
            for n in range(CROWS // 64):
                rows = pl.ds(aligned(j * CROWS + n * 64, 64), 64)
                value = g2[slot, rows, :].astype(jnp.float32) * norm[slot, 0:1, :]
                lhs[slot, n * 64 : (n + 1) * 64, :] = value.astype(jnp.bfloat16)
            return carry

        lax.fori_loop(0, 16, step, 0)

    def multiply_normed(j):
        gather_far(1, g2, j)
        normalize(j)
        pbuf[1, j] = product(lhs, rb2, 0, 1 - za).astype(jnp.bfloat16)
        partial_send(1, j).start()
        tq[j] = product(lhs, rb2, 0, za)

    def finished(j):
        partial_send(1, j).wait_recv()

        def finish(n, carry):
            rows = pl.ds(aligned(n * 32, 32), 32)
            out[pl.ds(aligned(j * CROWS + n * 32, 32), 32), :] = (
                tq[j, rows, :] + prec[1, j, rows, :].astype(jnp.float32)
            ).astype(jnp.bfloat16)
            return carry

        lax.fori_loop(0, CROWS // 32, finish, 0)

    coef_wait(1, rb2)
    multiply_normed(0)
    gather_near(1, g2, 2)
    multiply_normed(1)
    finished(0)
    multiply_normed(2)
    finished(1)
    finished(2)

    swap.wait_send()
    for j in range(CHUNKS):
        back(j).wait_send()
    for i, ext in ((0, oext), (1, dext)):
        for copy in rims(i, ext):
            copy.wait_send()
    for i, (g, r, rb) in enumerate(((g1, r1, rb1), (g2, r2, rb2))):
        gather_end(i, g)
        coef_end(i, r, rb)
        for j in range(CHUNKS):
            partial_send(i, j).wait_send()
    for step in range(1, 8):
        share(step).wait_send()
    for copy in norm_sends() + norm_forwards():
        copy.wait_send()


def shards(orbitals, potential, rot_first, rot_second):
    bf16, f32 = jnp.bfloat16, jnp.float32
    vmem = pl.BlockSpec(memory_space=pltpu.VMEM)
    dma = pltpu.SemaphoreType.DMA
    result = pl.pallas_call(
        kernel,
        out_shape=jax.ShapeDtypeStruct((ROWS, LANES), bf16),
        in_specs=[vmem] * 4,
        out_specs=vmem,
        scratch_shapes=[
            pltpu.VMEM((EXT * NY, HALF), bf16),
            pltpu.VMEM((EXT * NY, HALF), bf16),
            pltpu.VMEM((EXT, NY + 16, HALF), f32),
            pltpu.VMEM((GRID_X, NY), f32),
            pltpu.VMEM((PAIR, NY, HALF), f32),
            pltpu.VMEM((PAIR * NY, HALF), bf16),
            pltpu.VMEM((16, ROWS, LANES), bf16),
            pltpu.VMEM((16, ROWS, LANES), bf16),
            pltpu.VMEM((2, 4096, LANES), bf16),
            pltpu.VMEM((2, 4096, LANES), bf16),
            pltpu.VMEM((2, 1024, LANES), bf16),
            pltpu.VMEM((2, CHUNKS, CROWS, LANES), bf16),
            pltpu.VMEM((2, CHUNKS, CROWS, LANES), bf16),
            pltpu.VMEM((CHUNKS, CROWS, LANES), f32),
            pltpu.VMEM((8, 8, LANES), f32),
            pltpu.VMEM((16, 8, LANES), f32),
            pltpu.VMEM((16, CROWS, LANES), bf16),
            dma, dma,
            dma((CHUNKS,)), dma((CHUNKS,)),
            dma((1 + CHUNKS,)),
            dma((2, 2)), dma((2, 2)),
            dma((2, CHUNKS, 17)), dma((2, CHUNKS, 16)),
            dma((2, CHUNKS)), dma((2, CHUNKS)),
            dma((7,)), dma((7,)),
            dma((15,)), dma((16,)),
            dma((2, PIECES, 2)), dma((2, PIECES, 2)), dma((2, PIECES)),
            dma((2, 2, PIECES, 4)), dma((2, 2, PIECES, 4)),
        ],
        compiler_params=pltpu.CompilerParams(
            collective_id=0, has_side_effects=True, vmem_limit_bytes=56 << 20
        ),
    )(orbitals.reshape(ROWS, LANES), potential, rot_first, rot_second)
    return result.reshape(OWN, NY, LANES)


def solution(mesh):
    placed = (P("dom", None, "band"), P(), P("dom", "band"), P("dom", "band"))
    return jax.shard_map(
        shards, mesh=mesh, in_specs=placed, out_specs=P("dom", None, "band"), check_vma=False
    )
```

```python
import functools

import jax
import jax.numpy as jnp
from jax import lax
from jax.experimental import pallas as pl
from jax.experimental.pallas import tpu as pltpu
from jax.sharding import PartitionSpec as P

stencil_weights = (
    -5369.0 / 1800.0,
    12.0 / 7.0,
    -15.0 / 56.0,
    10.0 / 189.0,
    -1.0 / 112.0,
    2.0 / 1925.0,
    -1.0 / 16632.0,
)
filter_center = 3.8
filter_half = 3.3

MESH = pl.DeviceIdType.MESH
GRID_X = 96
NY = 64
OWN = 12
ROWS = OWN * NY
LANES = 256
HALF = 128
CHUNKS = 3
CROWS = ROWS // CHUNKS
PAIR = 2 * OWN
EXT = PAIR + 12
CELLS = GRID_X * NY
PIECES = 2


SCHEDULE = {
    "start": "z00",
    "swap": "z01",
    "rim0": "n00",
    "back": "n01",
    "stay": "z10",
    "own02": "f00 f01",
    "pair02": "z11 n10",
    "mul00": "n11",
    "turn2": "f10 f11",
}


def aligned(value, multiple):
    return pl.multiple_of(value, multiple)


def kernel(
    orb, pot, r1, r2, out,
    oext, dext, vpad, potf, volt, filt, g1, g2, rb1, rb2, pbuf, prec, tq, sq, norm, lhs,
    swap_s, swap_r, back_s, back_r, loc, halo_s, halo_r,
    g_s, g_r, p_s, p_r, sq_s, sq_r, n_s, n_r, rz_s, rz_r, ry_s, ry_r,
):
    band = lax.axis_index("band")
    dom = lax.axis_index("dom")
    x = band // 8
    zl = (band // 2) % 4
    za = zl // 2
    zb = zl % 2
    core = band % 2
    y = dom // 2
    zh = dom % 2

    def device(x_=None, y_=None, zh_=None, za_=None, zb_=None, core_=None):
        pick = lambda new, old: old if new is None else new
        b = pick(x_, x) * 8 + (pick(za_, za) * 2 + pick(zb_, zb)) * 2 + pick(core_, core)
        d = pick(y_, y) * 2 + pick(zh_, zh)
        return {"band": b, "dom": d}

    def around(value, step):
        return (value + step) % 4

    def remote(src, dst, send, recv, to):
        return pltpu.make_async_remote_copy(
            src_ref=src, dst_ref=dst, send_sem=send, recv_sem=recv, device_id=to, device_id_type=MESH
        )

    barrier = pltpu.get_barrier_semaphore()
    partners = []
    for step in range(1, 8):
        z = (zh * 4 + zl + step) % 8
        partners.append(device(zh_=z // 4, za_=(z // 2) % 2, zb_=z % 2))
    for step in range(1, 4):
        partners.append(device(x_=around(x, step)))
        partners.append(device(y_=around(y, step)))
        partners.append(device(y_=around(y, step), zh_=1 - zh))
        partners.append(device(x_=around(x, step), za_=1 - za))
    partners.append(device(core_=1 - core))
    for to in partners:
        pl.semaphore_signal(barrier, inc=1, device_id=to, device_id_type=MESH)
    pl.semaphore_wait(barrier, len(partners))

    mine = aligned(zh * HALF, HALF)
    theirs = aligned((1 - zh) * HALF, HALF)
    own_at = aligned((6 + OWN * zh) * NY, NY)
    partner_at = aligned((6 + OWN * (1 - zh)) * NY, NY)
    swap = remote(
        orb.at[:, pl.ds(theirs, HALF)], oext.at[pl.ds(own_at, ROWS)], swap_s, swap_r, device(zh_=1 - zh)
    )
    swap.start()
    keep = pltpu.make_async_copy(orb.at[:, pl.ds(mine, HALF)], oext.at[pl.ds(own_at, ROWS)], loc.at[0])
    keep.start()

    def coef_z(i, r, rb, q):
        copies = []
        for n, (other_half, other_zb) in enumerate(((0, 0), (0, 1), (1, 0), (1, 1))):
            to_zb = (zb + other_zb) % 2
            source = r.at[pl.ds(aligned(to_zb * 512 + q * 256, 256), 256)]
            place = rb.at[zb, pl.ds(aligned(((y * 2 + q) * 2 + zh) * 256, 256), 256)]
            arrival = rz_r.at[i, q, zh * 2 + zb]
            if n == 0:
                copies.append(pltpu.make_async_copy(source, place, arrival))
            else:
                to = device(zh_=(zh + other_half) % 2, zb_=to_zb)
                copies.append(remote(source, place, rz_s.at[i, q, n - 1], arrival, to))
        return copies

    def coef_z_start(i, r, rb, q):
        for copy in coef_z(i, r, rb, q):
            copy.start()

    def ring(i, rb, part, q, n, step, to, first=0, count=512):
        rows = pl.ds(aligned((around(y, step) * 2 + q) * 512 + first, 256), count)
        return remote(
            rb.at[part, rows], rb.at[part, rows], ry_s.at[i, part, q, n], ry_r.at[i, part, q, n],
            device(y_=around(y, to)),
        )

    def coef_near(i, rb, q):
        return [ring(i, rb, part, q, n, 0, to) for part in range(2) for n, to in ((0, 1), (1, 3))]

    def coef_far(i, rb, q):
        return [
            ring(i, rb, part, q, n, step, to, first, 256)
            for part in range(2)
            for n, step, to, first in ((2, 3, 1, 0), (3, 1, 3, 256))
        ]

    def coef_near_start(i, r, rb, q):
        for half in range(2):
            for part in range(2):
                place = rb.at[part, pl.ds(aligned(((y * 2 + q) * 2 + half) * 256, 256), 256)]
                pltpu.make_async_copy(r.at[pl.ds(0, 256)], place, rz_r.at[i, q, half * 2 + part]).wait()
        for copy in coef_near(i, rb, q):
            copy.start()

    def coef_far_start(i, rb, q):
        for copy in coef_near(i, rb, q):
            copy.wait_recv()
        for copy in coef_far(i, rb, q):
            copy.start()

    def coef_wait(i, rb):
        for q in range(PIECES):
            for copy in coef_far(i, rb, q):
                copy.wait_recv()

    def coef_end(i, r, rb):
        for q in range(PIECES):
            for copy in coef_z(i, r, rb, q)[1:] + coef_near(i, rb, q) + coef_far(i, rb, q):
                copy.wait_send()

    rotations = ((r1, rb1), (r2, rb2))

    def at(point):
        for word in SCHEDULE.get(point, "").split():
            i, q = int(word[1]), int(word[2])
            r, rb = rotations[i]
            if word[0] == "z":
                coef_z_start(i, r, rb, q)
            elif word[0] == "n":
                coef_near_start(i, r, rb, q)
            else:
                coef_far_start(i, rb, q)

    at("start")

    diagonal = lax.broadcasted_iota(jnp.int32, (NY, NY), 0) == lax.broadcasted_iota(jnp.int32, (NY, NY), 1)
    ones = jnp.ones((NY, HALF), jnp.bfloat16)

    potf[...] = pot[...].astype(jnp.float32)

    def spread(i, carry):
        row = potf[pl.ds(y * PAIR + i, 1), :]
        square = jnp.where(diagonal, jnp.broadcast_to(row, (NY, NY)), 0.0).astype(jnp.bfloat16)
        volt[i] = jnp.dot(square, ones, preferred_element_type=jnp.float32)
        return carry

    lax.fori_loop(0, PAIR, spread, 0)

    def clear(i, carry):
        vpad[i, 0:8, :] = jnp.zeros((8, HALF), jnp.float32)
        vpad[i, 72:80, :] = jnp.zeros((8, HALF), jnp.float32)
        return carry

    lax.fori_loop(0, EXT, clear, 0)

    def rims(i, ext):
        up = remote(
            ext.at[pl.ds(24 * NY, 6 * NY)], ext.at[pl.ds(0, 6 * NY)], halo_s.at[i, 0], halo_r.at[i, 0],
            device(y_=around(y, 1)),
        )
        down = remote(
            ext.at[pl.ds(6 * NY, 6 * NY)], ext.at[pl.ds(30 * NY, 6 * NY)], halo_s.at[i, 1], halo_r.at[i, 1],
            device(y_=around(y, 3)),
        )
        return up, down

    def widen(ext, first, count, keep_it):
        def step(i, carry):
            at = first + i
            value = ext[pl.ds(aligned(at * NY, NY), NY), :].astype(jnp.float32)
            if keep_it is not None:
                value = jnp.where(keep_it, value, 0.0)
            vpad[at, 8:72, :] = value
            return carry

        lax.fori_loop(0, count, step, 0)

    def applied(i):
        center = vpad[i + 6, 8:72, :]
        lap = 2.0 * stencil_weights[0] * center
        for k in range(1, 7):
            lap = lap + stencil_weights[k] * (
                (vpad[i + 6 + k, 8:72, :] + vpad[i + 6 - k, 8:72, :])
                + (vpad[i + 6, 8 + k : 72 + k, :] + vpad[i + 6, 8 - k : 72 - k, :])
            )
        return -0.5 * lap + volt[i] * center, center

    at("volt")
    keep.wait()
    swap.wait_recv()
    for copy in rims(0, oext):
        copy.start()
    at("swap")
    widen(oext, 6, PAIR, None)
    for copy in rims(0, oext):
        copy.wait_recv()
    widen(oext, 0, 6, y > 0)
    widen(oext, 30, 6, y < 3)
    at("rim0")

    def first(i, carry):
        value, center = applied(i)
        dext[pl.ds(aligned((i + 6) * NY, NY), NY), :] = (
            (value - filter_center * center) * (1.0 / filter_half)
        ).astype(jnp.bfloat16)
        return carry

    lax.fori_loop(0, PAIR, first, 0)
    for copy in rims(1, dext):
        copy.start()
    at("first")
    widen(dext, 6, PAIR, None)
    for copy in rims(1, dext):
        copy.wait_recv()
    widen(dext, 0, 6, y > 0)
    widen(dext, 30, 6, y < 3)
    at("rim1")

    def second(i, carry):
        value, center = applied(i)
        start = oext[pl.ds(aligned((i + 6) * NY, NY), NY), :].astype(jnp.float32)
        filt[pl.ds(aligned(i * NY, NY), NY), :] = (
            (value - filter_center * center) * (2.0 / filter_half) - start
        ).astype(jnp.bfloat16)
        return carry

    own_slot = (x * 2 + core) * 2 + za
    half_lanes = pl.ds(mine, HALF)

    def back(j):
        source = filt.at[pl.ds(aligned((1 - zh) * ROWS + j * CROWS, CROWS), CROWS)]
        place = g1.at[own_slot, pl.ds(j * CROWS, CROWS), half_lanes]
        return remote(source, place, back_s.at[j], back_r.at[j], device(zh_=1 - zh))

    def stay(j):
        source = filt.at[pl.ds(aligned(zh * ROWS + j * CROWS, CROWS), CROWS)]
        place = g1.at[own_slot, pl.ds(j * CROWS, CROWS), half_lanes]
        return pltpu.make_async_copy(source, place, loc.at[1 + j])

    per = OWN // CHUNKS
    for j in range(CHUNKS):
        lax.fori_loop((1 - zh) * OWN + j * per, (1 - zh) * OWN + (j + 1) * per, second, 0)
        back(j).start()
    at("back")
    for j in range(CHUNKS):
        lax.fori_loop(zh * OWN + j * per, zh * OWN + (j + 1) * per, second, 0)
        stay(j).start()

    other_core = device(core_=1 - core)

    def block(g, slot, j):
        return g.at[slot, pl.ds(aligned(j * CROWS, CROWS), CROWS)]

    def send(i, g, slot, j, n, to):
        return remote(block(g, slot, j), block(g, slot, j), g_s.at[i, j, n], g_r.at[i, j, slot], to)

    right, left = device(x_=around(x, 1)), device(x_=around(x, 3))

    def slot_at(step, b):
        return (around(x, step) * 2 + core) * 2 + b

    def own_sends(i, g, j):
        return [send(i, g, own_slot, j, n, to) for n, to in enumerate((device(za_=1 - za), right, left, other_core))]

    def pair_sends(i, g, j):
        return [send(i, g, slot_at(0, 1 - za), j, 4 + n, to) for n, to in enumerate((right, left, other_core))]

    def near_sends(i, g, j):
        sends = []
        for step, first, to in ((3, 0, right), (1, CROWS // 2, left)):
            for b in (0, 1):
                slot = slot_at(step, b)
                rows = pl.ds(aligned(j * CROWS + first, CROWS // 2), CROWS // 2)
                part = g.at[slot, rows]
                n = 7 + len(sends)
                sends.append(remote(part, part, g_s.at[i, j, n], g_r.at[i, j, slot], to))
                sends.append(send(i, g, slot, j, n + 1, other_core))
        return sends

    def far_sends(i, g, j):
        return [send(i, g, slot_at(2, b), j, 15 + b, other_core) for b in (0, 1)]

    def arrived(i, g, slot, j):
        send(i, g, slot, j, 0, other_core).wait_recv()

    def gather_own(i, g, j):
        for copy in own_sends(i, g, j):
            copy.start()

    def gather_pair(i, g, j):
        arrived(i, g, slot_at(0, 1 - za), j)
        for copy in pair_sends(i, g, j):
            copy.start()

    def gather_near(i, g, j):
        for step in (3, 1):
            for b in (0, 1):
                arrived(i, g, slot_at(step, b), j)
        for copy in near_sends(i, g, j):
            copy.start()

    def gather_far(i, g, j):
        for b in (0, 1):
            arrived(i, g, slot_at(2, b), j)
        for copy in far_sends(i, g, j):
            copy.start()
        for slot in range(8):
            arrived(i, g, ((slot // 2) * 2 + 1 - core) * 2 + slot % 2, j)

    def gather_end(i, g):
        def step(j, carry):
            for copy in own_sends(i, g, j) + pair_sends(i, g, j) + near_sends(i, g, j) + far_sends(i, g, j):
                copy.wait_send()
            return carry

        lax.fori_loop(0, CHUNKS, step, 0)

    def product(g, rb, j, part):
        rows = pl.ds(aligned(j * CROWS, CROWS), CROWS)
        total = None
        for slot in range(16):
            term = jnp.dot(
                g[slot, rows, :], rb[part, slot * LANES : (slot + 1) * LANES, :], preferred_element_type=jnp.float32
            )
            total = term if total is None else total + term
        return total

    def partial_send(i, j):
        return remote(pbuf.at[i, j], prec.at[i, j], p_s.at[i, j], p_r.at[i, j], device(zb_=1 - zb))

    def multiply(i, g, rb, j):
        gather_far(i, g, j)
        pbuf[i, j] = product(g, rb, j, 1 - zb).astype(jnp.bfloat16)
        partial_send(i, j).start()
        tq[j] = product(g, rb, j, zb)

    at("stay")
    for j in range(CHUNKS):
        stay(j).wait()
        back(j).wait_recv()
        gather_own(0, g1, j)
        at(f"own0{j}")
    for j in range(CHUNKS):
        gather_pair(0, g1, j)
        at(f"pair0{j}")
    gather_near(0, g1, 0)
    at("near00")
    gather_near(0, g1, 1)
    at("near01")
    coef_wait(0, rb1)
    multiply(0, g1, rb1, 0)
    at("mul00")
    gather_near(0, g1, 2)
    at("near02")
    multiply(0, g1, rb1, 1)
    at("mul01")

    def turned(j, sums):
        partial_send(0, j).wait_recv()

        def step(n, total):
            rows = pl.ds(aligned(n * 32, 32), 32)
            value = tq[j, rows, :] + prec[0, j, rows, :].astype(jnp.float32)
            g2[own_slot, pl.ds(aligned(j * CROWS + n * 32, 32), 32), :] = value.astype(jnp.bfloat16)
            return total + jnp.sum((value * value).reshape(4, 8, LANES), axis=0)

        sums = lax.fori_loop(0, CROWS // 32, step, sums)
        gather_own(1, g2, j)
        return sums

    sums = turned(0, jnp.zeros((8, LANES), jnp.float32))
    at("turn0")
    multiply(0, g1, rb1, 2)
    at("mul02")
    sums = turned(1, sums)
    at("turn1")
    gather_pair(1, g2, 0)
    at("pair10")
    sums = turned(2, sums)
    at("turn2")
    sq[dom] = sums

    def share(step):
        to = (dom + step) % 8
        return remote(sq.at[dom], sq.at[dom], sq_s.at[step - 1], sq_r.at[step - 1], {"band": band, "dom": to})

    for step in range(1, 8):
        share(step).start()
    for step in range(1, 8):
        share(step).wait_recv()
    total = sq[0]
    for d in range(1, 8):
        total = total + sq[d]
    mean_square = jnp.sum(total, axis=0, keepdims=True) * (1.0 / CELLS)
    norm[own_slot] = jnp.broadcast_to(1.0 / jnp.sqrt(mean_square + 1e-06), (8, LANES))

    def norm_send(slot, n, to):
        return remote(norm.at[slot], norm.at[slot], n_s.at[n], n_r.at[slot], to)

    others = [(step, b) for step in range(4) for b in (0, 1) if step or b]

    def norm_sends():
        sends = [norm_send(own_slot, 0, other_core)]
        for n, (step, b) in enumerate(others):
            sends.append(norm_send(own_slot, 1 + n, device(x_=around(x, step), za_=(za + b) % 2)))
        return sends

    def norm_forwards():
        return [
            norm_send(slot_at(step, (za + b) % 2), 8 + n, other_core) for n, (step, b) in enumerate(others)
        ]

    for copy in norm_sends():
        copy.start()
    at("norm")
    gather_pair(1, g2, 1)
    at("pair11")
    gather_near(1, g2, 0)
    at("near10")
    gather_pair(1, g2, 2)
    at("pair12")
    for copy in norm_forwards():
        copy.wait_recv()
        copy.start()
    gather_near(1, g2, 1)
    at("near11")
    for slot in range(8):
        norm_send(((slot // 2) * 2 + 1 - core) * 2 + slot % 2, 0, other_core).wait_recv()

    def normalize(j):
        def step(slot, carry):
            for n in range(CROWS // 64):
                rows = pl.ds(aligned(j * CROWS + n * 64, 64), 64)
                value = g2[slot, rows, :].astype(jnp.float32) * norm[slot, 0:1, :]
                lhs[slot, n * 64 : (n + 1) * 64, :] = value.astype(jnp.bfloat16)
            return carry

        lax.fori_loop(0, 16, step, 0)

    def multiply_normed(j):
        gather_far(1, g2, j)
        normalize(j)
        pbuf[1, j] = product(lhs, rb2, 0, 1 - zb).astype(jnp.bfloat16)
        partial_send(1, j).start()
        tq[j] = product(lhs, rb2, 0, zb)

    def finished(j):
        partial_send(1, j).wait_recv()

        def finish(n, carry):
            rows = pl.ds(aligned(n * 32, 32), 32)
            out[pl.ds(aligned(j * CROWS + n * 32, 32), 32), :] = (
                tq[j, rows, :] + prec[1, j, rows, :].astype(jnp.float32)
            ).astype(jnp.bfloat16)
            return carry

        lax.fori_loop(0, CROWS // 32, finish, 0)

    coef_wait(1, rb2)
    multiply_normed(0)
    gather_near(1, g2, 2)
    multiply_normed(1)
    finished(0)
    multiply_normed(2)
    finished(1)
    finished(2)

    swap.wait_send()
    for j in range(CHUNKS):
        back(j).wait_send()
    for i, ext in ((0, oext), (1, dext)):
        for copy in rims(i, ext):
            copy.wait_send()
    for i, (g, r, rb) in enumerate(((g1, r1, rb1), (g2, r2, rb2))):
        gather_end(i, g)
        coef_end(i, r, rb)
        for j in range(CHUNKS):
            partial_send(i, j).wait_send()
    for step in range(1, 8):
        share(step).wait_send()
    for copy in norm_sends() + norm_forwards():
        copy.wait_send()


def shards(orbitals, potential, rot_first, rot_second):
    bf16, f32 = jnp.bfloat16, jnp.float32
    vmem = pl.BlockSpec(memory_space=pltpu.VMEM)
    dma = pltpu.SemaphoreType.DMA
    result = pl.pallas_call(
        kernel,
        out_shape=jax.ShapeDtypeStruct((ROWS, LANES), bf16),
        in_specs=[vmem] * 4,
        out_specs=vmem,
        scratch_shapes=[
            pltpu.VMEM((EXT * NY, HALF), bf16),
            pltpu.VMEM((EXT * NY, HALF), bf16),
            pltpu.VMEM((EXT, NY + 16, HALF), f32),
            pltpu.VMEM((GRID_X, NY), f32),
            pltpu.VMEM((PAIR, NY, HALF), f32),
            pltpu.VMEM((PAIR * NY, HALF), bf16),
            pltpu.VMEM((16, ROWS, LANES), bf16),
            pltpu.VMEM((16, ROWS, LANES), bf16),
            pltpu.VMEM((2, 4096, LANES), bf16),
            pltpu.VMEM((2, 4096, LANES), bf16),
            pltpu.VMEM((2, CHUNKS, CROWS, LANES), bf16),
            pltpu.VMEM((2, CHUNKS, CROWS, LANES), bf16),
            pltpu.VMEM((CHUNKS, CROWS, LANES), f32),
            pltpu.VMEM((8, 8, LANES), f32),
            pltpu.VMEM((16, 8, LANES), f32),
            pltpu.VMEM((16, CROWS, LANES), bf16),
            dma, dma,
            dma((CHUNKS,)), dma((CHUNKS,)),
            dma((1 + CHUNKS,)),
            dma((2, 2)), dma((2, 2)),
            dma((2, CHUNKS, 17)), dma((2, CHUNKS, 16)),
            dma((2, CHUNKS)), dma((2, CHUNKS)),
            dma((7,)), dma((7,)),
            dma((15,)), dma((16,)),
            dma((2, PIECES, 3)), dma((2, PIECES, 4)),
            dma((2, 2, PIECES, 4)), dma((2, 2, PIECES, 4)),
        ],
        compiler_params=pltpu.CompilerParams(
            collective_id=0, has_side_effects=True, vmem_limit_bytes=56 << 20
        ),
    )(orbitals.reshape(ROWS, LANES), potential, rot_first, rot_second)
    return result.reshape(OWN, NY, LANES)


def solution(mesh):
    placed = (P("dom", None, "band"), P(), P("dom", "band"), P("dom", "band"))
    return jax.shard_map(
        shards, mesh=mesh, in_specs=placed, out_specs=P("dom", None, "band"), check_vma=False
    )
```

```python
import functools

import jax
import jax.numpy as jnp
from jax import lax
from jax.experimental import pallas as pl
from jax.experimental.pallas import tpu as pltpu
from jax.sharding import PartitionSpec as P

stencil_weights = (
    -5369.0 / 1800.0,
    12.0 / 7.0,
    -15.0 / 56.0,
    10.0 / 189.0,
    -1.0 / 112.0,
    2.0 / 1925.0,
    -1.0 / 16632.0,
)
filter_center = 3.8
filter_half = 3.3

MESH = pl.DeviceIdType.MESH
GRID_X = 96
NY = 64
OWN = 12
ROWS = OWN * NY
LANES = 256
HALF = 128
CHUNKS = 3
CROWS = ROWS // CHUNKS
PAIR = 2 * OWN
EXT = PAIR + 12
CELLS = GRID_X * NY
PIECES = 2


SCHEDULE = {
    "start": "z00 z01",
    "rim0": "z10",
    "back": "n00",
    "stay": "n01",
    "own02": "f00 f01",
    "pair02": "z11 n10",
    "mul00": "n11",
    "share": "f10",
    "pair11": "f11",
}


def aligned(value, multiple):
    return pl.multiple_of(value, multiple)


def kernel(
    orb, pot, r1, r2, out,
    oext, dext, vpad, potf, volt, filt, g1, g2, rb1, rb2, pbuf, prec, tq, sq, norm, lhs,
    swap_s, swap_r, back_s, back_r, loc, halo_s, halo_r,
    g_s, g_r, p_s, p_r, sq_s, sq_r, n_s, n_r, rz_s, rz_r, ry_s, ry_r,
):
    band = lax.axis_index("band")
    dom = lax.axis_index("dom")
    x = band // 8
    zl = (band // 2) % 4
    za = zl // 2
    zb = zl % 2
    core = band % 2
    y = dom // 2
    zh = dom % 2

    def device(x_=None, y_=None, zh_=None, za_=None, zb_=None, core_=None):
        pick = lambda new, old: old if new is None else new
        b = pick(x_, x) * 8 + (pick(za_, za) * 2 + pick(zb_, zb)) * 2 + pick(core_, core)
        d = pick(y_, y) * 2 + pick(zh_, zh)
        return {"band": b, "dom": d}

    def around(value, step):
        return (value + step) % 4

    def remote(src, dst, send, recv, to):
        return pltpu.make_async_remote_copy(
            src_ref=src, dst_ref=dst, send_sem=send, recv_sem=recv, device_id=to, device_id_type=MESH
        )

    barrier = pltpu.get_barrier_semaphore()
    partners = []
    for step in range(1, 8):
        z = (zh * 4 + zl + step) % 8
        partners.append(device(zh_=z // 4, za_=(z // 2) % 2, zb_=z % 2))
    for step in range(1, 4):
        partners.append(device(x_=around(x, step)))
        partners.append(device(y_=around(y, step)))
        partners.append(device(y_=around(y, step), zh_=1 - zh))
        partners.append(device(x_=around(x, step), za_=1 - za))
    partners.append(device(core_=1 - core))
    for to in partners:
        pl.semaphore_signal(barrier, inc=1, device_id=to, device_id_type=MESH)
    pl.semaphore_wait(barrier, len(partners))

    mine = aligned(zh * HALF, HALF)
    theirs = aligned((1 - zh) * HALF, HALF)
    own_at = aligned((6 + OWN * zh) * NY, NY)
    partner_at = aligned((6 + OWN * (1 - zh)) * NY, NY)
    swap = remote(
        orb.at[:, pl.ds(theirs, HALF)], oext.at[pl.ds(own_at, ROWS)], swap_s, swap_r, device(zh_=1 - zh)
    )
    swap.start()
    keep = pltpu.make_async_copy(orb.at[:, pl.ds(mine, HALF)], oext.at[pl.ds(own_at, ROWS)], loc.at[0])
    keep.start()

    def coef_z(i, r, rb, q):
        copies = []
        for n, (other_half, other_zb) in enumerate(((0, 0), (0, 1), (1, 0), (1, 1))):
            to_zb = (zb + other_zb) % 2
            source = r.at[pl.ds(aligned(to_zb * 512 + q * 256, 256), 256)]
            place = rb.at[zb, pl.ds(aligned(((y * 2 + q) * 2 + zh) * 256, 256), 256)]
            arrival = rz_r.at[i, q, zh * 2 + zb]
            if n == 0:
                copies.append(pltpu.make_async_copy(source, place, arrival))
            else:
                to = device(zh_=(zh + other_half) % 2, zb_=to_zb)
                copies.append(remote(source, place, rz_s.at[i, q, n - 1], arrival, to))
        return copies

    def coef_z_start(i, r, rb, q):
        for copy in coef_z(i, r, rb, q):
            copy.start()

    def ring(i, rb, part, q, n, step, to, first=0, count=512):
        rows = pl.ds(aligned((around(y, step) * 2 + q) * 512 + first, 256), count)
        return remote(
            rb.at[part, rows], rb.at[part, rows], ry_s.at[i, part, q, n], ry_r.at[i, part, q, n],
            device(y_=around(y, to)),
        )

    def coef_near(i, rb, q):
        return [ring(i, rb, part, q, n, 0, to) for part in range(2) for n, to in ((0, 1), (1, 3))]

    def coef_far(i, rb, q):
        return [
            ring(i, rb, part, q, n, step, to, first, 256)
            for part in range(2)
            for n, step, to, first in ((2, 3, 1, 0), (3, 1, 3, 256))
        ]

    def coef_near_start(i, r, rb, q):
        for half in range(2):
            for part in range(2):
                place = rb.at[part, pl.ds(aligned(((y * 2 + q) * 2 + half) * 256, 256), 256)]
                pltpu.make_async_copy(r.at[pl.ds(0, 256)], place, rz_r.at[i, q, half * 2 + part]).wait()
        for copy in coef_near(i, rb, q):
            copy.start()

    def coef_far_start(i, rb, q):
        for copy in coef_near(i, rb, q):
            copy.wait_recv()
        for copy in coef_far(i, rb, q):
            copy.start()

    def coef_wait(i, rb):
        for q in range(PIECES):
            for copy in coef_far(i, rb, q):
                copy.wait_recv()

    def coef_end(i, r, rb):
        for q in range(PIECES):
            for copy in coef_z(i, r, rb, q)[1:] + coef_near(i, rb, q) + coef_far(i, rb, q):
                copy.wait_send()

    rotations = ((r1, rb1), (r2, rb2))

    def at(point):
        for word in SCHEDULE.get(point, "").split():
            i, q = int(word[1]), int(word[2])
            r, rb = rotations[i]
            if word[0] == "z":
                coef_z_start(i, r, rb, q)
            elif word[0] == "n":
                coef_near_start(i, r, rb, q)
            else:
                coef_far_start(i, rb, q)

    at("start")

    diagonal = lax.broadcasted_iota(jnp.int32, (NY, NY), 0) == lax.broadcasted_iota(jnp.int32, (NY, NY), 1)
    ones = jnp.ones((NY, HALF), jnp.bfloat16)

    potf[...] = pot[...].astype(jnp.float32)

    def spread(i, carry):
        row = potf[pl.ds(y * PAIR + i, 1), :]
        square = jnp.where(diagonal, jnp.broadcast_to(row, (NY, NY)), 0.0).astype(jnp.bfloat16)
        volt[i] = jnp.dot(square, ones, preferred_element_type=jnp.float32)
        return carry

    lax.fori_loop(0, PAIR, spread, 0)

    def clear(i, carry):
        vpad[i, 0:8, :] = jnp.zeros((8, HALF), jnp.float32)
        vpad[i, 72:80, :] = jnp.zeros((8, HALF), jnp.float32)
        return carry

    lax.fori_loop(0, EXT, clear, 0)

    def rims(i, ext):
        up = remote(
            ext.at[pl.ds(24 * NY, 6 * NY)], ext.at[pl.ds(0, 6 * NY)], halo_s.at[i, 0], halo_r.at[i, 0],
            device(y_=around(y, 1)),
        )
        down = remote(
            ext.at[pl.ds(6 * NY, 6 * NY)], ext.at[pl.ds(30 * NY, 6 * NY)], halo_s.at[i, 1], halo_r.at[i, 1],
            device(y_=around(y, 3)),
        )
        return up, down

    def widen(ext, first, count, keep_it):
        def step(i, carry):
            at = first + i
            value = ext[pl.ds(aligned(at * NY, NY), NY), :].astype(jnp.float32)
            if keep_it is not None:
                value = jnp.where(keep_it, value, 0.0)
            vpad[at, 8:72, :] = value
            return carry

        lax.fori_loop(0, count, step, 0)

    def applied(i):
        center = vpad[i + 6, 8:72, :]
        lap = 2.0 * stencil_weights[0] * center
        for k in range(1, 7):
            lap = lap + stencil_weights[k] * (
                (vpad[i + 6 + k, 8:72, :] + vpad[i + 6 - k, 8:72, :])
                + (vpad[i + 6, 8 + k : 72 + k, :] + vpad[i + 6, 8 - k : 72 - k, :])
            )
        return -0.5 * lap + volt[i] * center, center

    at("volt")
    keep.wait()
    swap.wait_recv()
    for copy in rims(0, oext):
        copy.start()
    at("swap")
    widen(oext, 6, PAIR, None)
    for copy in rims(0, oext):
        copy.wait_recv()
    widen(oext, 0, 6, y > 0)
    widen(oext, 30, 6, y < 3)
    at("rim0")

    def first(i, carry):
        value, center = applied(i)
        dext[pl.ds(aligned((i + 6) * NY, NY), NY), :] = (
            (value - filter_center * center) * (1.0 / filter_half)
        ).astype(jnp.bfloat16)
        return carry

    lax.fori_loop(0, PAIR, first, 0)
    for copy in rims(1, dext):
        copy.start()
    at("first")
    widen(dext, 6, PAIR, None)
    for copy in rims(1, dext):
        copy.wait_recv()
    widen(dext, 0, 6, y > 0)
    widen(dext, 30, 6, y < 3)
    at("rim1")

    def second(i, carry):
        value, center = applied(i)
        start = oext[pl.ds(aligned((i + 6) * NY, NY), NY), :].astype(jnp.float32)
        filt[pl.ds(aligned(i * NY, NY), NY), :] = (
            (value - filter_center * center) * (2.0 / filter_half) - start
        ).astype(jnp.bfloat16)
        return carry

    own_slot = (x * 2 + core) * 2 + za
    half_lanes = pl.ds(mine, HALF)

    def back(j):
        source = filt.at[pl.ds(aligned((1 - zh) * ROWS + j * CROWS, CROWS), CROWS)]
        place = g1.at[own_slot, pl.ds(j * CROWS, CROWS), half_lanes]
        return remote(source, place, back_s.at[j], back_r.at[j], device(zh_=1 - zh))

    def stay(j):
        source = filt.at[pl.ds(aligned(zh * ROWS + j * CROWS, CROWS), CROWS)]
        place = g1.at[own_slot, pl.ds(j * CROWS, CROWS), half_lanes]
        return pltpu.make_async_copy(source, place, loc.at[1 + j])

    per = OWN // CHUNKS
    for j in range(CHUNKS):
        lax.fori_loop((1 - zh) * OWN + j * per, (1 - zh) * OWN + (j + 1) * per, second, 0)
        back(j).start()
    at("back")
    for j in range(CHUNKS):
        lax.fori_loop(zh * OWN + j * per, zh * OWN + (j + 1) * per, second, 0)
        stay(j).start()

    other_core = device(core_=1 - core)

    def block(g, slot, j):
        return g.at[slot, pl.ds(aligned(j * CROWS, CROWS), CROWS)]

    def send(i, g, slot, j, n, to):
        return remote(block(g, slot, j), block(g, slot, j), g_s.at[i, j, n], g_r.at[i, j, slot], to)

    right, left = device(x_=around(x, 1)), device(x_=around(x, 3))

    def slot_at(step, b):
        return (around(x, step) * 2 + core) * 2 + b

    def own_sends(i, g, j):
        return [send(i, g, own_slot, j, n, to) for n, to in enumerate((device(za_=1 - za), right, left, other_core))]

    def pair_sends(i, g, j):
        return [send(i, g, slot_at(0, 1 - za), j, 4 + n, to) for n, to in enumerate((right, left, other_core))]

    def near_sends(i, g, j):
        sends = []
        for step, first, to in ((3, 0, right), (1, CROWS // 2, left)):
            for b in (0, 1):
                slot = slot_at(step, b)
                rows = pl.ds(aligned(j * CROWS + first, CROWS // 2), CROWS // 2)
                part = g.at[slot, rows]
                n = 7 + len(sends)
                sends.append(remote(part, part, g_s.at[i, j, n], g_r.at[i, j, slot], to))
                sends.append(send(i, g, slot, j, n + 1, other_core))
        return sends

    def far_sends(i, g, j):
        return [send(i, g, slot_at(2, b), j, 15 + b, other_core) for b in (0, 1)]

    def arrived(i, g, slot, j):
        send(i, g, slot, j, 0, other_core).wait_recv()

    def gather_own(i, g, j):
        for copy in own_sends(i, g, j):
            copy.start()

    def gather_pair(i, g, j):
        arrived(i, g, slot_at(0, 1 - za), j)
        for copy in pair_sends(i, g, j):
            copy.start()

    def gather_near(i, g, j):
        for step in (3, 1):
            for b in (0, 1):
                arrived(i, g, slot_at(step, b), j)
        for copy in near_sends(i, g, j):
            copy.start()

    def gather_far(i, g, j):
        for b in (0, 1):
            arrived(i, g, slot_at(2, b), j)
        for copy in far_sends(i, g, j):
            copy.start()
        for slot in range(8):
            arrived(i, g, ((slot // 2) * 2 + 1 - core) * 2 + slot % 2, j)

    def gather_end(i, g):
        def step(j, carry):
            for copy in own_sends(i, g, j) + pair_sends(i, g, j) + near_sends(i, g, j) + far_sends(i, g, j):
                copy.wait_send()
            return carry

        lax.fori_loop(0, CHUNKS, step, 0)

    def product(g, rb, j, part):
        rows = pl.ds(aligned(j * CROWS, CROWS), CROWS)
        total = None
        for slot in range(16):
            term = jnp.dot(
                g[slot, rows, :], rb[part, slot * LANES : (slot + 1) * LANES, :], preferred_element_type=jnp.float32
            )
            total = term if total is None else total + term
        return total

    def partial_send(i, j):
        return remote(pbuf.at[i, j], prec.at[i, j], p_s.at[i, j], p_r.at[i, j], device(zb_=1 - zb))

    def multiply(i, g, rb, j):
        gather_far(i, g, j)
        pbuf[i, j] = product(g, rb, j, 1 - zb).astype(jnp.bfloat16)
        partial_send(i, j).start()
        tq[j] = product(g, rb, j, zb)

    at("stay")
    for j in range(CHUNKS):
        stay(j).wait()
        back(j).wait_recv()
        gather_own(0, g1, j)
        at(f"own0{j}")
    for j in range(CHUNKS):
        gather_pair(0, g1, j)
        at(f"pair0{j}")
    gather_near(0, g1, 0)
    at("near00")
    gather_near(0, g1, 1)
    at("near01")
    coef_wait(0, rb1)
    multiply(0, g1, rb1, 0)
    at("mul00")
    gather_near(0, g1, 2)
    at("near02")
    multiply(0, g1, rb1, 1)
    at("mul01")

    def turned(j, sums):
        partial_send(0, j).wait_recv()

        def step(n, total):
            rows = pl.ds(aligned(n * 32, 32), 32)
            value = tq[j, rows, :] + prec[0, j, rows, :].astype(jnp.float32)
            g2[own_slot, pl.ds(aligned(j * CROWS + n * 32, 32), 32), :] = value.astype(jnp.bfloat16)
            return total + jnp.sum((value * value).reshape(4, 8, LANES), axis=0)

        sums = lax.fori_loop(0, CROWS // 32, step, sums)
        gather_own(1, g2, j)
        return sums

    sums = turned(0, jnp.zeros((8, LANES), jnp.float32))
    at("turn0")
    multiply(0, g1, rb1, 2)
    at("mul02")
    sums = turned(1, sums)
    at("turn1")
    gather_pair(1, g2, 0)
    at("pair10")
    sums = turned(2, sums)
    sq[dom] = sums

    def share(step):
        to = (dom + step) % 8
        return remote(sq.at[dom], sq.at[dom], sq_s.at[step - 1], sq_r.at[step - 1], {"band": band, "dom": to})

    for step in range(1, 8):
        share(step).start()
    at("share")
    gather_pair(1, g2, 1)
    at("pair11")
    for step in range(1, 8):
        share(step).wait_recv()
    total = sq[0]
    for d in range(1, 8):
        total = total + sq[d]
    mean_square = jnp.sum(total, axis=0, keepdims=True) * (1.0 / CELLS)
    norm[own_slot] = jnp.broadcast_to(1.0 / jnp.sqrt(mean_square + 1e-06), (8, LANES))

    def norm_send(slot, n, to):
        return remote(norm.at[slot], norm.at[slot], n_s.at[n], n_r.at[slot], to)

    others = [(step, b) for step in range(4) for b in (0, 1) if step or b]

    def norm_sends():
        sends = [norm_send(own_slot, 0, other_core)]
        for n, (step, b) in enumerate(others):
            sends.append(norm_send(own_slot, 1 + n, device(x_=around(x, step), za_=(za + b) % 2)))
        return sends

    def norm_forwards():
        return [
            norm_send(slot_at(step, (za + b) % 2), 8 + n, other_core) for n, (step, b) in enumerate(others)
        ]

    for copy in norm_sends():
        copy.start()
    at("norm")
    gather_near(1, g2, 0)
    at("near10")
    gather_pair(1, g2, 2)
    at("pair12")
    for copy in norm_forwards():
        copy.wait_recv()
        copy.start()
    gather_near(1, g2, 1)
    at("near11")
    for slot in range(8):
        norm_send(((slot // 2) * 2 + 1 - core) * 2 + slot % 2, 0, other_core).wait_recv()

    def normalize(j):
        def step(slot, carry):
            for n in range(CROWS // 64):
                rows = pl.ds(aligned(j * CROWS + n * 64, 64), 64)
                value = g2[slot, rows, :].astype(jnp.float32) * norm[slot, 0:1, :]
                lhs[slot, n * 64 : (n + 1) * 64, :] = value.astype(jnp.bfloat16)
            return carry

        lax.fori_loop(0, 16, step, 0)

    def multiply_normed(j):
        gather_far(1, g2, j)
        normalize(j)
        pbuf[1, j] = product(lhs, rb2, 0, 1 - zb).astype(jnp.bfloat16)
        partial_send(1, j).start()
        tq[j] = product(lhs, rb2, 0, zb)

    def finished(j):
        partial_send(1, j).wait_recv()

        def finish(n, carry):
            rows = pl.ds(aligned(n * 32, 32), 32)
            out[pl.ds(aligned(j * CROWS + n * 32, 32), 32), :] = (
                tq[j, rows, :] + prec[1, j, rows, :].astype(jnp.float32)
            ).astype(jnp.bfloat16)
            return carry

        lax.fori_loop(0, CROWS // 32, finish, 0)

    coef_wait(1, rb2)
    multiply_normed(0)
    gather_near(1, g2, 2)
    multiply_normed(1)
    finished(0)
    multiply_normed(2)
    finished(1)
    finished(2)

    swap.wait_send()
    for j in range(CHUNKS):
        back(j).wait_send()
    for i, ext in ((0, oext), (1, dext)):
        for copy in rims(i, ext):
            copy.wait_send()
    for i, (g, r, rb) in enumerate(((g1, r1, rb1), (g2, r2, rb2))):
        gather_end(i, g)
        coef_end(i, r, rb)
        for j in range(CHUNKS):
            partial_send(i, j).wait_send()
    for step in range(1, 8):
        share(step).wait_send()
    for copy in norm_sends() + norm_forwards():
        copy.wait_send()


def shards(orbitals, potential, rot_first, rot_second):
    bf16, f32 = jnp.bfloat16, jnp.float32
    vmem = pl.BlockSpec(memory_space=pltpu.VMEM)
    dma = pltpu.SemaphoreType.DMA
    result = pl.pallas_call(
        kernel,
        out_shape=jax.ShapeDtypeStruct((ROWS, LANES), bf16),
        in_specs=[vmem] * 4,
        out_specs=vmem,
        scratch_shapes=[
            pltpu.VMEM((EXT * NY, HALF), bf16),
            pltpu.VMEM((EXT * NY, HALF), bf16),
            pltpu.VMEM((EXT, NY + 16, HALF), f32),
            pltpu.VMEM((GRID_X, NY), f32),
            pltpu.VMEM((PAIR, NY, HALF), f32),
            pltpu.VMEM((PAIR * NY, HALF), bf16),
            pltpu.VMEM((16, ROWS, LANES), bf16),
            pltpu.VMEM((16, ROWS, LANES), bf16),
            pltpu.VMEM((2, 4096, LANES), bf16),
            pltpu.VMEM((2, 4096, LANES), bf16),
            pltpu.VMEM((2, CHUNKS, CROWS, LANES), bf16),
            pltpu.VMEM((2, CHUNKS, CROWS, LANES), bf16),
            pltpu.VMEM((CHUNKS, CROWS, LANES), f32),
            pltpu.VMEM((8, 8, LANES), f32),
            pltpu.VMEM((16, 8, LANES), f32),
            pltpu.VMEM((16, CROWS, LANES), bf16),
            dma, dma,
            dma((CHUNKS,)), dma((CHUNKS,)),
            dma((1 + CHUNKS,)),
            dma((2, 2)), dma((2, 2)),
            dma((2, CHUNKS, 17)), dma((2, CHUNKS, 16)),
            dma((2, CHUNKS)), dma((2, CHUNKS)),
            dma((7,)), dma((7,)),
            dma((15,)), dma((16,)),
            dma((2, PIECES, 3)), dma((2, PIECES, 4)),
            dma((2, 2, PIECES, 4)), dma((2, 2, PIECES, 4)),
        ],
        compiler_params=pltpu.CompilerParams(
            collective_id=0, has_side_effects=True, vmem_limit_bytes=56 << 20
        ),
    )(orbitals.reshape(ROWS, LANES), potential, rot_first, rot_second)
    return result.reshape(OWN, NY, LANES)


def solution(mesh):
    placed = (P("dom", None, "band"), P(), P("dom", "band"), P("dom", "band"))
    return jax.shard_map(
        shards, mesh=mesh, in_specs=placed, out_specs=P("dom", None, "band"), check_vma=False
    )
```

```python
import functools

import jax
import jax.numpy as jnp
from jax import lax
from jax.experimental import pallas as pl
from jax.experimental.pallas import tpu as pltpu
from jax.sharding import PartitionSpec as P

stencil_weights = (
    -5369.0 / 1800.0,
    12.0 / 7.0,
    -15.0 / 56.0,
    10.0 / 189.0,
    -1.0 / 112.0,
    2.0 / 1925.0,
    -1.0 / 16632.0,
)
filter_center = 3.8
filter_half = 3.3

MESH = pl.DeviceIdType.MESH
GRID_X = 96
NY = 64
OWN = 12
ROWS = OWN * NY
LANES = 256
HALF = 128
CHUNKS = 3
CROWS = ROWS // CHUNKS
PAIR = 2 * OWN
EXT = PAIR + 12
CELLS = GRID_X * NY
PIECES = 2


SCHEDULE = {
    "start": "z00 z01",
    "first": "z10",
    "back": "n00",
    "stay": "n01",
    "own02": "f00 f01",
    "pair02": "z11 n10",
    "mul00": "n11",
    "share": "f10",
    "pair11": "f11",
}


def aligned(value, multiple):
    return pl.multiple_of(value, multiple)


def kernel(
    orb, pot, r1, r2, out,
    oext, dext, vpad, potf, volt, filt, g1, g2, rb1, rb2, pbuf, prec, tq, sq, norm, lhs,
    swap_s, swap_r, back_s, back_r, loc, halo_s, halo_r,
    g_s, g_r, p_s, p_r, sq_s, sq_r, n_s, n_r, rz_s, rz_r, ry_s, ry_r,
):
    band = lax.axis_index("band")
    dom = lax.axis_index("dom")
    x = band // 8
    zl = (band // 2) % 4
    za = zl // 2
    zb = zl % 2
    core = band % 2
    y = dom // 2
    zh = dom % 2

    def device(x_=None, y_=None, zh_=None, za_=None, zb_=None, core_=None):
        pick = lambda new, old: old if new is None else new
        b = pick(x_, x) * 8 + (pick(za_, za) * 2 + pick(zb_, zb)) * 2 + pick(core_, core)
        d = pick(y_, y) * 2 + pick(zh_, zh)
        return {"band": b, "dom": d}

    def around(value, step):
        return (value + step) % 4

    def remote(src, dst, send, recv, to):
        return pltpu.make_async_remote_copy(
            src_ref=src, dst_ref=dst, send_sem=send, recv_sem=recv, device_id=to, device_id_type=MESH
        )

    barrier = pltpu.get_barrier_semaphore()
    partners = []
    for step in range(1, 8):
        z = (zh * 4 + zl + step) % 8
        partners.append(device(zh_=z // 4, za_=(z // 2) % 2, zb_=z % 2))
    for step in range(1, 4):
        partners.append(device(x_=around(x, step)))
        partners.append(device(y_=around(y, step)))
        partners.append(device(y_=around(y, step), zh_=1 - zh))
        partners.append(device(x_=around(x, step), za_=1 - za))
    partners.append(device(core_=1 - core))
    for to in partners:
        pl.semaphore_signal(barrier, inc=1, device_id=to, device_id_type=MESH)
    pl.semaphore_wait(barrier, len(partners))

    mine = aligned(zh * HALF, HALF)
    theirs = aligned((1 - zh) * HALF, HALF)
    own_at = aligned((6 + OWN * zh) * NY, NY)
    partner_at = aligned((6 + OWN * (1 - zh)) * NY, NY)
    swap = remote(
        orb.at[:, pl.ds(theirs, HALF)], oext.at[pl.ds(own_at, ROWS)], swap_s, swap_r, device(zh_=1 - zh)
    )
    swap.start()
    keep = pltpu.make_async_copy(orb.at[:, pl.ds(mine, HALF)], oext.at[pl.ds(own_at, ROWS)], loc.at[0])
    keep.start()

    def coef_z(i, r, rb, q):
        copies = []
        for n, (other_half, other_zb) in enumerate(((0, 0), (0, 1), (1, 0), (1, 1))):
            to_zb = (zb + other_zb) % 2
            source = r.at[pl.ds(aligned(to_zb * 512 + q * 256, 256), 256)]
            place = rb.at[zb, pl.ds(aligned(((y * 2 + q) * 2 + zh) * 256, 256), 256)]
            arrival = rz_r.at[i, q, zh * 2 + zb]
            if n == 0:
                copies.append(pltpu.make_async_copy(source, place, arrival))
            else:
                to = device(zh_=(zh + other_half) % 2, zb_=to_zb)
                copies.append(remote(source, place, rz_s.at[i, q, n - 1], arrival, to))
        return copies

    def coef_z_start(i, r, rb, q):
        for copy in coef_z(i, r, rb, q):
            copy.start()

    def ring(i, rb, part, q, n, step, to, first=0, count=512):
        rows = pl.ds(aligned((around(y, step) * 2 + q) * 512 + first, 256), count)
        return remote(
            rb.at[part, rows], rb.at[part, rows], ry_s.at[i, part, q, n], ry_r.at[i, part, q, n],
            device(y_=around(y, to)),
        )

    def coef_near(i, rb, q):
        return [ring(i, rb, part, q, n, 0, to) for part in range(2) for n, to in ((0, 1), (1, 3))]

    def coef_far(i, rb, q):
        return [
            ring(i, rb, part, q, n, step, to, first, 256)
            for part in range(2)
            for n, step, to, first in ((2, 3, 1, 0), (3, 1, 3, 256))
        ]

    def coef_near_start(i, r, rb, q):
        for half in range(2):
            for part in range(2):
                place = rb.at[part, pl.ds(aligned(((y * 2 + q) * 2 + half) * 256, 256), 256)]
                pltpu.make_async_copy(r.at[pl.ds(0, 256)], place, rz_r.at[i, q, half * 2 + part]).wait()
        for copy in coef_near(i, rb, q):
            copy.start()

    def coef_far_start(i, rb, q):
        for copy in coef_near(i, rb, q):
            copy.wait_recv()
        for copy in coef_far(i, rb, q):
            copy.start()

    def coef_wait(i, rb):
        for q in range(PIECES):
            for copy in coef_far(i, rb, q):
                copy.wait_recv()

    def coef_end(i, r, rb):
        for q in range(PIECES):
            for copy in coef_z(i, r, rb, q)[1:] + coef_near(i, rb, q) + coef_far(i, rb, q):
                copy.wait_send()

    rotations = ((r1, rb1), (r2, rb2))

    def at(point):
        for word in SCHEDULE.get(point, "").split():
            i, q = int(word[1]), int(word[2])
            r, rb = rotations[i]
            if word[0] == "z":
                coef_z_start(i, r, rb, q)
            elif word[0] == "n":
                coef_near_start(i, r, rb, q)
            else:
                coef_far_start(i, rb, q)

    at("start")

    diagonal = lax.broadcasted_iota(jnp.int32, (NY, NY), 0) == lax.broadcasted_iota(jnp.int32, (NY, NY), 1)
    ones = jnp.ones((NY, HALF), jnp.bfloat16)

    potf[...] = pot[...].astype(jnp.float32)

    def spread(i, carry):
        row = potf[pl.ds(y * PAIR + i, 1), :]
        square = jnp.where(diagonal, jnp.broadcast_to(row, (NY, NY)), 0.0).astype(jnp.bfloat16)
        volt[i] = jnp.dot(square, ones, preferred_element_type=jnp.float32)
        return carry

    lax.fori_loop(0, PAIR, spread, 0)

    def clear(i, carry):
        vpad[i, 0:8, :] = jnp.zeros((8, HALF), jnp.float32)
        vpad[i, 72:80, :] = jnp.zeros((8, HALF), jnp.float32)
        return carry

    lax.fori_loop(0, EXT, clear, 0)

    def rims(i, ext):
        up = remote(
            ext.at[pl.ds(24 * NY, 6 * NY)], ext.at[pl.ds(0, 6 * NY)], halo_s.at[i, 0], halo_r.at[i, 0],
            device(y_=around(y, 1)),
        )
        down = remote(
            ext.at[pl.ds(6 * NY, 6 * NY)], ext.at[pl.ds(30 * NY, 6 * NY)], halo_s.at[i, 1], halo_r.at[i, 1],
            device(y_=around(y, 3)),
        )
        return up, down

    def widen(ext, first, count, keep_it):
        def step(i, carry):
            at = first + i
            value = ext[pl.ds(aligned(at * NY, NY), NY), :].astype(jnp.float32)
            if keep_it is not None:
                value = jnp.where(keep_it, value, 0.0)
            vpad[at, 8:72, :] = value
            return carry

        lax.fori_loop(0, count, step, 0)

    def applied(i):
        center = vpad[i + 6, 8:72, :]
        lap = 2.0 * stencil_weights[0] * center
        for k in range(1, 7):
            lap = lap + stencil_weights[k] * (
                (vpad[i + 6 + k, 8:72, :] + vpad[i + 6 - k, 8:72, :])
                + (vpad[i + 6, 8 + k : 72 + k, :] + vpad[i + 6, 8 - k : 72 - k, :])
            )
        return -0.5 * lap + volt[i] * center, center

    at("volt")
    keep.wait()
    swap.wait_recv()
    for copy in rims(0, oext):
        copy.start()
    at("swap")
    widen(oext, 6, PAIR, None)
    for copy in rims(0, oext):
        copy.wait_recv()
    widen(oext, 0, 6, y > 0)
    widen(oext, 30, 6, y < 3)
    at("rim0")

    def first(i, carry):
        value, center = applied(i)
        dext[pl.ds(aligned((i + 6) * NY, NY), NY), :] = (
            (value - filter_center * center) * (1.0 / filter_half)
        ).astype(jnp.bfloat16)
        return carry

    lax.fori_loop(0, PAIR, first, 0)
    for copy in rims(1, dext):
        copy.start()
    at("first")
    widen(dext, 6, PAIR, None)
    for copy in rims(1, dext):
        copy.wait_recv()
    widen(dext, 0, 6, y > 0)
    widen(dext, 30, 6, y < 3)
    at("rim1")

    def second(i, carry):
        value, center = applied(i)
        start = oext[pl.ds(aligned((i + 6) * NY, NY), NY), :].astype(jnp.float32)
        filt[pl.ds(aligned(i * NY, NY), NY), :] = (
            (value - filter_center * center) * (2.0 / filter_half) - start
        ).astype(jnp.bfloat16)
        return carry

    own_slot = (x * 2 + core) * 2 + za
    half_lanes = pl.ds(mine, HALF)

    def back(j):
        source = filt.at[pl.ds(aligned((1 - zh) * ROWS + j * CROWS, CROWS), CROWS)]
        place = g1.at[own_slot, pl.ds(j * CROWS, CROWS), half_lanes]
        return remote(source, place, back_s.at[j], back_r.at[j], device(zh_=1 - zh))

    def stay(j):
        source = filt.at[pl.ds(aligned(zh * ROWS + j * CROWS, CROWS), CROWS)]
        place = g1.at[own_slot, pl.ds(j * CROWS, CROWS), half_lanes]
        return pltpu.make_async_copy(source, place, loc.at[1 + j])

    per = OWN // CHUNKS
    for j in range(CHUNKS):
        lax.fori_loop((1 - zh) * OWN + j * per, (1 - zh) * OWN + (j + 1) * per, second, 0)
        back(j).start()
    at("back")
    for j in range(CHUNKS):
        lax.fori_loop(zh * OWN + j * per, zh * OWN + (j + 1) * per, second, 0)
        stay(j).start()

    other_core = device(core_=1 - core)

    def block(g, slot, j):
        return g.at[slot, pl.ds(aligned(j * CROWS, CROWS), CROWS)]

    def send(i, g, slot, j, n, to):
        return remote(block(g, slot, j), block(g, slot, j), g_s.at[i, j, n], g_r.at[i, j, slot], to)

    right, left = device(x_=around(x, 1)), device(x_=around(x, 3))

    def slot_at(step, b):
        return (around(x, step) * 2 + core) * 2 + b

    def own_sends(i, g, j):
        return [send(i, g, own_slot, j, n, to) for n, to in enumerate((device(za_=1 - za), right, left, other_core))]

    def pair_sends(i, g, j):
        return [send(i, g, slot_at(0, 1 - za), j, 4 + n, to) for n, to in enumerate((right, left, other_core))]

    def near_sends(i, g, j):
        sends = []
        for step, first, to in ((3, 0, right), (1, CROWS // 2, left)):
            for b in (0, 1):
                slot = slot_at(step, b)
                rows = pl.ds(aligned(j * CROWS + first, CROWS // 2), CROWS // 2)
                part = g.at[slot, rows]
                n = 7 + len(sends)
                sends.append(remote(part, part, g_s.at[i, j, n], g_r.at[i, j, slot], to))
                sends.append(send(i, g, slot, j, n + 1, other_core))
        return sends

    def far_sends(i, g, j):
        return [send(i, g, slot_at(2, b), j, 15 + b, other_core) for b in (0, 1)]

    def arrived(i, g, slot, j):
        send(i, g, slot, j, 0, other_core).wait_recv()

    def gather_own(i, g, j):
        for copy in own_sends(i, g, j):
            copy.start()

    def gather_pair(i, g, j):
        arrived(i, g, slot_at(0, 1 - za), j)
        for copy in pair_sends(i, g, j):
            copy.start()

    def gather_near(i, g, j):
        for step in (3, 1):
            for b in (0, 1):
                arrived(i, g, slot_at(step, b), j)
        for copy in near_sends(i, g, j):
            copy.start()

    def gather_far(i, g, j):
        for b in (0, 1):
            arrived(i, g, slot_at(2, b), j)
        for copy in far_sends(i, g, j):
            copy.start()
        for slot in range(8):
            arrived(i, g, ((slot // 2) * 2 + 1 - core) * 2 + slot % 2, j)

    def gather_end(i, g):
        def step(j, carry):
            for copy in own_sends(i, g, j) + pair_sends(i, g, j) + near_sends(i, g, j) + far_sends(i, g, j):
                copy.wait_send()
            return carry

        lax.fori_loop(0, CHUNKS, step, 0)

    def product(g, rb, j, part):
        rows = pl.ds(aligned(j * CROWS, CROWS), CROWS)
        total = None
        for slot in range(16):
            term = jnp.dot(
                g[slot, rows, :], rb[part, slot * LANES : (slot + 1) * LANES, :], preferred_element_type=jnp.float32
            )
            total = term if total is None else total + term
        return total

    def partial_send(i, j):
        return remote(pbuf.at[i, j], prec.at[i, j], p_s.at[i, j], p_r.at[i, j], device(zb_=1 - zb))

    def multiply(i, g, rb, j):
        pbuf[i, j] = product(g, rb, j, 1 - zb).astype(jnp.bfloat16)
        partial_send(i, j).start()
        tq[j] = product(g, rb, j, zb)

    at("stay")
    for j in range(CHUNKS):
        stay(j).wait()
        back(j).wait_recv()
        gather_own(0, g1, j)
        at(f"own0{j}")
    for j in range(CHUNKS):
        gather_pair(0, g1, j)
        at(f"pair0{j}")
    gather_near(0, g1, 0)
    at("near00")
    gather_near(0, g1, 1)
    at("near01")
    gather_far(0, g1, 0)
    gather_near(0, g1, 2)
    at("near02")
    gather_far(0, g1, 1)
    at("far01")
    coef_wait(0, rb1)
    multiply(0, g1, rb1, 0)
    at("mul00")
    multiply(0, g1, rb1, 1)
    at("mul01")

    def turned(j, sums):
        partial_send(0, j).wait_recv()

        def step(n, total):
            rows = pl.ds(aligned(n * 32, 32), 32)
            value = tq[j, rows, :] + prec[0, j, rows, :].astype(jnp.float32)
            g2[own_slot, pl.ds(aligned(j * CROWS + n * 32, 32), 32), :] = value.astype(jnp.bfloat16)
            return total + jnp.sum((value * value).reshape(4, 8, LANES), axis=0)

        sums = lax.fori_loop(0, CROWS // 32, step, sums)
        gather_own(1, g2, j)
        return sums

    sums = turned(0, jnp.zeros((8, LANES), jnp.float32))
    at("turn0")
    gather_far(0, g1, 2)
    multiply(0, g1, rb1, 2)
    at("mul02")
    sums = turned(1, sums)
    at("turn1")
    gather_pair(1, g2, 0)
    at("pair10")
    sums = turned(2, sums)
    sq[dom] = sums

    def share(step):
        to = (dom + step) % 8
        return remote(sq.at[dom], sq.at[dom], sq_s.at[step - 1], sq_r.at[step - 1], {"band": band, "dom": to})

    for step in range(1, 8):
        share(step).start()
    at("share")
    gather_pair(1, g2, 1)
    at("pair11")
    for step in range(1, 8):
        share(step).wait_recv()
    total = sq[0]
    for d in range(1, 8):
        total = total + sq[d]
    mean_square = jnp.sum(total, axis=0, keepdims=True) * (1.0 / CELLS)
    norm[own_slot] = jnp.broadcast_to(1.0 / jnp.sqrt(mean_square + 1e-06), (8, LANES))

    def norm_send(slot, n, to):
        return remote(norm.at[slot], norm.at[slot], n_s.at[n], n_r.at[slot], to)

    others = [(step, b) for step in range(4) for b in (0, 1) if step or b]

    def norm_sends():
        sends = [norm_send(own_slot, 0, other_core)]
        for n, (step, b) in enumerate(others):
            sends.append(norm_send(own_slot, 1 + n, device(x_=around(x, step), za_=(za + b) % 2)))
        return sends

    def norm_forwards():
        return [
            norm_send(slot_at(step, (za + b) % 2), 8 + n, other_core) for n, (step, b) in enumerate(others)
        ]

    for copy in norm_sends():
        copy.start()
    at("norm")
    gather_near(1, g2, 0)
    at("near10")
    gather_pair(1, g2, 2)
    at("pair12")
    for copy in norm_forwards():
        copy.wait_recv()
        copy.start()
    gather_near(1, g2, 1)
    at("near11")
    for slot in range(8):
        norm_send(((slot // 2) * 2 + 1 - core) * 2 + slot % 2, 0, other_core).wait_recv()

    def normalize(j):
        def step(slot, carry):
            for n in range(CROWS // 64):
                rows = pl.ds(aligned(j * CROWS + n * 64, 64), 64)
                value = g2[slot, rows, :].astype(jnp.float32) * norm[slot, 0:1, :]
                lhs[slot, n * 64 : (n + 1) * 64, :] = value.astype(jnp.bfloat16)
            return carry

        lax.fori_loop(0, 16, step, 0)

    def multiply_normed(j):
        pbuf[1, j] = product(lhs, rb2, 0, 1 - zb).astype(jnp.bfloat16)
        partial_send(1, j).start()
        tq[j] = product(lhs, rb2, 0, zb)

    def finished(j):
        partial_send(1, j).wait_recv()

        def finish(n, carry):
            rows = pl.ds(aligned(n * 32, 32), 32)
            out[pl.ds(aligned(j * CROWS + n * 32, 32), 32), :] = (
                tq[j, rows, :] + prec[1, j, rows, :].astype(jnp.float32)
            ).astype(jnp.bfloat16)
            return carry

        lax.fori_loop(0, CROWS // 32, finish, 0)

    gather_far(1, g2, 0)
    normalize(0)
    coef_wait(1, rb2)
    multiply_normed(0)
    gather_near(1, g2, 2)
    gather_far(1, g2, 1)
    normalize(1)
    multiply_normed(1)
    finished(0)
    gather_far(1, g2, 2)
    normalize(2)
    multiply_normed(2)
    finished(1)
    finished(2)

    swap.wait_send()
    for j in range(CHUNKS):
        back(j).wait_send()
    for i, ext in ((0, oext), (1, dext)):
        for copy in rims(i, ext):
            copy.wait_send()
    for i, (g, r, rb) in enumerate(((g1, r1, rb1), (g2, r2, rb2))):
        gather_end(i, g)
        coef_end(i, r, rb)
        for j in range(CHUNKS):
            partial_send(i, j).wait_send()
    for step in range(1, 8):
        share(step).wait_send()
    for copy in norm_sends() + norm_forwards():
        copy.wait_send()


def shards(orbitals, potential, rot_first, rot_second):
    bf16, f32 = jnp.bfloat16, jnp.float32
    vmem = pl.BlockSpec(memory_space=pltpu.VMEM)
    dma = pltpu.SemaphoreType.DMA
    result = pl.pallas_call(
        kernel,
        out_shape=jax.ShapeDtypeStruct((ROWS, LANES), bf16),
        in_specs=[vmem] * 4,
        out_specs=vmem,
        scratch_shapes=[
            pltpu.VMEM((EXT * NY, HALF), bf16),
            pltpu.VMEM((EXT * NY, HALF), bf16),
            pltpu.VMEM((EXT, NY + 16, HALF), f32),
            pltpu.VMEM((GRID_X, NY), f32),
            pltpu.VMEM((PAIR, NY, HALF), f32),
            pltpu.VMEM((PAIR * NY, HALF), bf16),
            pltpu.VMEM((16, ROWS, LANES), bf16),
            pltpu.VMEM((16, ROWS, LANES), bf16),
            pltpu.VMEM((2, 4096, LANES), bf16),
            pltpu.VMEM((2, 4096, LANES), bf16),
            pltpu.VMEM((2, CHUNKS, CROWS, LANES), bf16),
            pltpu.VMEM((2, CHUNKS, CROWS, LANES), bf16),
            pltpu.VMEM((CHUNKS, CROWS, LANES), f32),
            pltpu.VMEM((8, 8, LANES), f32),
            pltpu.VMEM((16, 8, LANES), f32),
            pltpu.VMEM((16, CROWS, LANES), bf16),
            dma, dma,
            dma((CHUNKS,)), dma((CHUNKS,)),
            dma((1 + CHUNKS,)),
            dma((2, 2)), dma((2, 2)),
            dma((2, CHUNKS, 17)), dma((2, CHUNKS, 16)),
            dma((2, CHUNKS)), dma((2, CHUNKS)),
            dma((7,)), dma((7,)),
            dma((15,)), dma((16,)),
            dma((2, PIECES, 3)), dma((2, PIECES, 4)),
            dma((2, 2, PIECES, 4)), dma((2, 2, PIECES, 4)),
        ],
        compiler_params=pltpu.CompilerParams(
            collective_id=0, has_side_effects=True, vmem_limit_bytes=56 << 20
        ),
    )(orbitals.reshape(ROWS, LANES), potential, rot_first, rot_second)
    return result.reshape(OWN, NY, LANES)


def solution(mesh):
    placed = (P("dom", None, "band"), P(), P("dom", "band"), P("dom", "band"))
    return jax.shard_map(
        shards, mesh=mesh, in_specs=placed, out_specs=P("dom", None, "band"), check_vma=False
    )
```

```python
import functools

import jax
import jax.numpy as jnp
from jax import lax
from jax.experimental import pallas as pl
from jax.experimental.pallas import tpu as pltpu
from jax.sharding import PartitionSpec as P

stencil_weights = (
    -5369.0 / 1800.0,
    12.0 / 7.0,
    -15.0 / 56.0,
    10.0 / 189.0,
    -1.0 / 112.0,
    2.0 / 1925.0,
    -1.0 / 16632.0,
)
filter_center = 3.8
filter_half = 3.3

MESH = pl.DeviceIdType.MESH
GRID_X = 96
NY = 64
OWN = 12
ROWS = OWN * NY
LANES = 256
HALF = 128
CHUNKS = 3
CROWS = ROWS // CHUNKS
PAIR = 2 * OWN
EXT = PAIR + 12
CELLS = GRID_X * NY
PIECES = 2


SCHEDULE = {
    "start": "z00 z01",
    "first": "z10",
    "back": "n00",
    "stay": "n01",
    "own02": "f00 f01",
    "pair02": "z11 n10",
    "mul00": "n11",
    "share": "f10",
    "pair11": "f11",
}


def aligned(value, multiple):
    return pl.multiple_of(value, multiple)


def kernel(
    orb, pot, r1, r2, out,
    oext, dext, vpad, potf, volt, filt, g1, g2, rb1, rb2, pbuf, prec, tq, sq, norm, lhs,
    swap_s, swap_r, back_s, back_r, loc, halo_s, halo_r,
    g_s, g_r, p_s, p_r, sq_s, sq_r, n_s, n_r, rz_s, rz_r, ry_s, ry_r,
):
    band = lax.axis_index("band")
    dom = lax.axis_index("dom")
    x = band // 8
    zl = (band // 2) % 4
    za = zl // 2
    zb = zl % 2
    core = band % 2
    y = dom // 2
    zh = dom % 2

    def device(x_=None, y_=None, zh_=None, za_=None, zb_=None, core_=None):
        pick = lambda new, old: old if new is None else new
        b = pick(x_, x) * 8 + (pick(za_, za) * 2 + pick(zb_, zb)) * 2 + pick(core_, core)
        d = pick(y_, y) * 2 + pick(zh_, zh)
        return {"band": b, "dom": d}

    def around(value, step):
        return (value + step) % 4

    def remote(src, dst, send, recv, to):
        return pltpu.make_async_remote_copy(
            src_ref=src, dst_ref=dst, send_sem=send, recv_sem=recv, device_id=to, device_id_type=MESH
        )

    barrier = pltpu.get_barrier_semaphore()
    partners = []
    for step in range(1, 8):
        z = (zh * 4 + zl + step) % 8
        partners.append(device(zh_=z // 4, za_=(z // 2) % 2, zb_=z % 2))
    for step in range(1, 4):
        partners.append(device(x_=around(x, step)))
        partners.append(device(y_=around(y, step)))
        partners.append(device(y_=around(y, step), zh_=1 - zh))
        partners.append(device(x_=around(x, step), za_=1 - za))
    partners.append(device(core_=1 - core))
    for to in partners:
        pl.semaphore_signal(barrier, inc=1, device_id=to, device_id_type=MESH)
    pl.semaphore_wait(barrier, len(partners))

    mine = aligned(zh * HALF, HALF)
    theirs = aligned((1 - zh) * HALF, HALF)
    own_at = aligned((6 + OWN * zh) * NY, NY)
    partner_at = aligned((6 + OWN * (1 - zh)) * NY, NY)
    swap = remote(
        orb.at[:, pl.ds(theirs, HALF)], oext.at[pl.ds(own_at, ROWS)], swap_s, swap_r, device(zh_=1 - zh)
    )
    swap.start()
    keep = pltpu.make_async_copy(orb.at[:, pl.ds(mine, HALF)], oext.at[pl.ds(own_at, ROWS)], loc.at[0])
    keep.start()

    def coef_z(i, r, rb, q):
        copies = []
        for n, (other_half, other_zb) in enumerate(((0, 0), (0, 1), (1, 0), (1, 1))):
            to_zb = (zb + other_zb) % 2
            source = r.at[pl.ds(aligned(to_zb * 512 + q * 256, 256), 256)]
            place = rb.at[zb, pl.ds(aligned(((y * 2 + q) * 2 + zh) * 256, 256), 256)]
            arrival = rz_r.at[i, q, zh * 2 + zb]
            if n == 0:
                copies.append(pltpu.make_async_copy(source, place, arrival))
            else:
                to = device(zh_=(zh + other_half) % 2, zb_=to_zb)
                copies.append(remote(source, place, rz_s.at[i, q, n - 1], arrival, to))
        return copies

    def coef_z_start(i, r, rb, q):
        for copy in coef_z(i, r, rb, q):
            copy.start()

    def ring(i, rb, part, q, n, step, to, first=0, count=512):
        rows = pl.ds(aligned((around(y, step) * 2 + q) * 512 + first, 256), count)
        return remote(
            rb.at[part, rows], rb.at[part, rows], ry_s.at[i, part, q, n], ry_r.at[i, part, q, n],
            device(y_=around(y, to)),
        )

    def coef_near(i, rb, q):
        return [ring(i, rb, part, q, n, 0, to) for part in range(2) for n, to in ((0, 1), (1, 3))]

    def coef_far(i, rb, q):
        return [
            ring(i, rb, part, q, n, step, to, first, 256)
            for part in range(2)
            for n, step, to, first in ((2, 3, 1, 0), (3, 1, 3, 256))
        ]

    def coef_near_start(i, r, rb, q):
        for half in range(2):
            for part in range(2):
                place = rb.at[part, pl.ds(aligned(((y * 2 + q) * 2 + half) * 256, 256), 256)]
                pltpu.make_async_copy(r.at[pl.ds(0, 256)], place, rz_r.at[i, q, half * 2 + part]).wait()
        for copy in coef_near(i, rb, q):
            copy.start()

    def coef_far_start(i, rb, q):
        for copy in coef_near(i, rb, q):
            copy.wait_recv()
        for copy in coef_far(i, rb, q):
            copy.start()

    def coef_wait(i, rb):
        for q in range(PIECES):
            for copy in coef_far(i, rb, q):
                copy.wait_recv()

    def coef_end(i, r, rb):
        for q in range(PIECES):
            for copy in coef_z(i, r, rb, q)[1:] + coef_near(i, rb, q) + coef_far(i, rb, q):
                copy.wait_send()

    rotations = ((r1, rb1), (r2, rb2))

    def at(point):
        for word in SCHEDULE.get(point, "").split():
            i, q = int(word[1]), int(word[2])
            r, rb = rotations[i]
            if word[0] == "z":
                coef_z_start(i, r, rb, q)
            elif word[0] == "n":
                coef_near_start(i, r, rb, q)
            else:
                coef_far_start(i, rb, q)

    at("start")

    diagonal = lax.broadcasted_iota(jnp.int32, (NY, NY), 0) == lax.broadcasted_iota(jnp.int32, (NY, NY), 1)
    ones = jnp.ones((NY, HALF), jnp.bfloat16)

    potf[...] = pot[...].astype(jnp.float32)

    def spread(i, carry):
        row = potf[pl.ds(y * PAIR + i, 1), :]
        square = jnp.where(diagonal, jnp.broadcast_to(row, (NY, NY)), 0.0).astype(jnp.bfloat16)
        volt[i] = jnp.dot(square, ones, preferred_element_type=jnp.float32)
        return carry

    lax.fori_loop(0, PAIR, spread, 0)

    def clear(i, carry):
        vpad[i, 0:8, :] = jnp.zeros((8, HALF), jnp.float32)
        vpad[i, 72:80, :] = jnp.zeros((8, HALF), jnp.float32)
        return carry

    lax.fori_loop(0, EXT, clear, 0)

    def rims(i, ext):
        up = remote(
            ext.at[pl.ds(24 * NY, 6 * NY)], ext.at[pl.ds(0, 6 * NY)], halo_s.at[i, 0], halo_r.at[i, 0],
            device(y_=around(y, 1)),
        )
        down = remote(
            ext.at[pl.ds(6 * NY, 6 * NY)], ext.at[pl.ds(30 * NY, 6 * NY)], halo_s.at[i, 1], halo_r.at[i, 1],
            device(y_=around(y, 3)),
        )
        return up, down

    def widen(ext, first, count, keep_it):
        def step(i, carry):
            at = first + i
            value = ext[pl.ds(aligned(at * NY, NY), NY), :].astype(jnp.float32)
            if keep_it is not None:
                value = jnp.where(keep_it, value, 0.0)
            vpad[at, 8:72, :] = value
            return carry

        lax.fori_loop(0, count, step, 0, unroll=3)

    def applied(i):
        center = vpad[i + 6, 8:72, :]
        lap = 2.0 * stencil_weights[0] * center
        for k in range(1, 7):
            lap = lap + stencil_weights[k] * (
                (vpad[i + 6 + k, 8:72, :] + vpad[i + 6 - k, 8:72, :])
                + (vpad[i + 6, 8 + k : 72 + k, :] + vpad[i + 6, 8 - k : 72 - k, :])
            )
        return -0.5 * lap + volt[i] * center, center

    at("volt")
    keep.wait()
    swap.wait_recv()
    for copy in rims(0, oext):
        copy.start()
    at("swap")
    widen(oext, 6, PAIR, None)
    for copy in rims(0, oext):
        copy.wait_recv()
    widen(oext, 0, 6, y > 0)
    widen(oext, 30, 6, y < 3)
    at("rim0")

    def first(i, carry):
        value, center = applied(i)
        dext[pl.ds(aligned((i + 6) * NY, NY), NY), :] = (
            (value - filter_center * center) * (1.0 / filter_half)
        ).astype(jnp.bfloat16)
        return carry

    lax.fori_loop(0, PAIR, first, 0, unroll=2)
    for copy in rims(1, dext):
        copy.start()
    at("first")
    widen(dext, 6, PAIR, None)
    for copy in rims(1, dext):
        copy.wait_recv()
    widen(dext, 0, 6, y > 0)
    widen(dext, 30, 6, y < 3)
    at("rim1")

    def second(i, carry):
        value, center = applied(i)
        start = oext[pl.ds(aligned((i + 6) * NY, NY), NY), :].astype(jnp.float32)
        filt[pl.ds(aligned(i * NY, NY), NY), :] = (
            (value - filter_center * center) * (2.0 / filter_half) - start
        ).astype(jnp.bfloat16)
        return carry

    own_slot = (x * 2 + core) * 2 + za
    half_lanes = pl.ds(mine, HALF)

    def back(j):
        source = filt.at[pl.ds(aligned((1 - zh) * ROWS + j * CROWS, CROWS), CROWS)]
        place = g1.at[own_slot, pl.ds(j * CROWS, CROWS), half_lanes]
        return remote(source, place, back_s.at[j], back_r.at[j], device(zh_=1 - zh))

    def stay(j):
        source = filt.at[pl.ds(aligned(zh * ROWS + j * CROWS, CROWS), CROWS)]
        place = g1.at[own_slot, pl.ds(j * CROWS, CROWS), half_lanes]
        return pltpu.make_async_copy(source, place, loc.at[1 + j])

    per = OWN // CHUNKS
    for j in range(CHUNKS):
        lax.fori_loop((1 - zh) * OWN + j * per, (1 - zh) * OWN + (j + 1) * per, second, 0)
        back(j).start()
    at("back")
    for j in range(CHUNKS):
        lax.fori_loop(zh * OWN + j * per, zh * OWN + (j + 1) * per, second, 0)
        stay(j).start()

    other_core = device(core_=1 - core)

    def block(g, slot, j):
        return g.at[slot, pl.ds(aligned(j * CROWS, CROWS), CROWS)]

    def send(i, g, slot, j, n, to):
        return remote(block(g, slot, j), block(g, slot, j), g_s.at[i, j, n], g_r.at[i, j, slot], to)

    right, left = device(x_=around(x, 1)), device(x_=around(x, 3))

    def slot_at(step, b):
        return (around(x, step) * 2 + core) * 2 + b

    def own_sends(i, g, j):
        return [send(i, g, own_slot, j, n, to) for n, to in enumerate((device(za_=1 - za), right, left, other_core))]

    def pair_sends(i, g, j):
        return [send(i, g, slot_at(0, 1 - za), j, 4 + n, to) for n, to in enumerate((right, left, other_core))]

    def near_sends(i, g, j):
        sends = []
        for step, first, to in ((3, 0, right), (1, CROWS // 2, left)):
            for b in (0, 1):
                slot = slot_at(step, b)
                rows = pl.ds(aligned(j * CROWS + first, CROWS // 2), CROWS // 2)
                part = g.at[slot, rows]
                n = 7 + len(sends)
                sends.append(remote(part, part, g_s.at[i, j, n], g_r.at[i, j, slot], to))
                sends.append(send(i, g, slot, j, n + 1, other_core))
        return sends

    def far_sends(i, g, j):
        return [send(i, g, slot_at(2, b), j, 15 + b, other_core) for b in (0, 1)]

    def arrived(i, g, slot, j):
        send(i, g, slot, j, 0, other_core).wait_recv()

    def gather_own(i, g, j):
        for copy in own_sends(i, g, j):
            copy.start()

    def gather_pair(i, g, j):
        arrived(i, g, slot_at(0, 1 - za), j)
        for copy in pair_sends(i, g, j):
            copy.start()

    def gather_near(i, g, j):
        for step in (3, 1):
            for b in (0, 1):
                arrived(i, g, slot_at(step, b), j)
        for copy in near_sends(i, g, j):
            copy.start()

    def gather_far(i, g, j):
        for b in (0, 1):
            arrived(i, g, slot_at(2, b), j)
        for copy in far_sends(i, g, j):
            copy.start()
        for slot in range(8):
            arrived(i, g, ((slot // 2) * 2 + 1 - core) * 2 + slot % 2, j)

    def gather_end(i, g):
        def step(j, carry):
            for copy in own_sends(i, g, j) + pair_sends(i, g, j) + near_sends(i, g, j) + far_sends(i, g, j):
                copy.wait_send()
            return carry

        lax.fori_loop(0, CHUNKS, step, 0)

    def product(g, rb, j, part):
        rows = pl.ds(aligned(j * CROWS, CROWS), CROWS)
        total = None
        for slot in range(16):
            term = jnp.dot(
                g[slot, rows, :], rb[part, slot * LANES : (slot + 1) * LANES, :], preferred_element_type=jnp.float32
            )
            total = term if total is None else total + term
        return total

    def partial_send(i, j):
        return remote(pbuf.at[i, j], prec.at[i, j], p_s.at[i, j], p_r.at[i, j], device(zb_=1 - zb))

    def multiply(i, g, rb, j):
        pbuf[i, j] = product(g, rb, j, 1 - zb).astype(jnp.bfloat16)
        partial_send(i, j).start()
        tq[j] = product(g, rb, j, zb)

    at("stay")
    for j in range(CHUNKS):
        stay(j).wait()
        back(j).wait_recv()
        gather_own(0, g1, j)
        at(f"own0{j}")
    for j in range(CHUNKS):
        gather_pair(0, g1, j)
        at(f"pair0{j}")
    gather_near(0, g1, 0)
    at("near00")
    gather_near(0, g1, 1)
    at("near01")
    gather_far(0, g1, 0)
    gather_near(0, g1, 2)
    at("near02")
    gather_far(0, g1, 1)
    at("far01")
    coef_wait(0, rb1)
    multiply(0, g1, rb1, 0)
    at("mul00")
    multiply(0, g1, rb1, 1)
    at("mul01")

    def turned(j, sums):
        partial_send(0, j).wait_recv()

        def step(n, total):
            rows = pl.ds(aligned(n * 32, 32), 32)
            value = tq[j, rows, :] + prec[0, j, rows, :].astype(jnp.float32)
            g2[own_slot, pl.ds(aligned(j * CROWS + n * 32, 32), 32), :] = value.astype(jnp.bfloat16)
            return total + jnp.sum((value * value).reshape(4, 8, LANES), axis=0)

        sums = lax.fori_loop(0, CROWS // 32, step, sums, unroll=2)
        gather_own(1, g2, j)
        return sums

    sums = turned(0, jnp.zeros((8, LANES), jnp.float32))
    at("turn0")
    gather_far(0, g1, 2)
    multiply(0, g1, rb1, 2)
    at("mul02")
    sums = turned(1, sums)
    at("turn1")
    gather_pair(1, g2, 0)
    at("pair10")
    sums = turned(2, sums)
    sq[dom] = sums

    def share(step):
        to = (dom + step) % 8
        return remote(sq.at[dom], sq.at[dom], sq_s.at[step - 1], sq_r.at[step - 1], {"band": band, "dom": to})

    for step in range(1, 8):
        share(step).start()
    at("share")
    gather_pair(1, g2, 1)
    at("pair11")
    for step in range(1, 8):
        share(step).wait_recv()
    total = sq[0]
    for d in range(1, 8):
        total = total + sq[d]
    mean_square = jnp.sum(total, axis=0, keepdims=True) * (1.0 / CELLS)
    norm[own_slot] = jnp.broadcast_to(1.0 / jnp.sqrt(mean_square + 1e-06), (8, LANES))

    def norm_send(slot, n, to):
        return remote(norm.at[slot], norm.at[slot], n_s.at[n], n_r.at[slot], to)

    others = [(step, b) for step in range(4) for b in (0, 1) if step or b]

    def norm_sends():
        sends = [norm_send(own_slot, 0, other_core)]
        for n, (step, b) in enumerate(others):
            sends.append(norm_send(own_slot, 1 + n, device(x_=around(x, step), za_=(za + b) % 2)))
        return sends

    def norm_forwards():
        return [
            norm_send(slot_at(step, (za + b) % 2), 8 + n, other_core) for n, (step, b) in enumerate(others)
        ]

    for copy in norm_sends():
        copy.start()
    at("norm")
    gather_near(1, g2, 0)
    at("near10")
    gather_pair(1, g2, 2)
    at("pair12")
    for copy in norm_forwards():
        copy.wait_recv()
        copy.start()
    gather_near(1, g2, 1)
    at("near11")
    for slot in range(8):
        norm_send(((slot // 2) * 2 + 1 - core) * 2 + slot % 2, 0, other_core).wait_recv()

    def normalize(j):
        def step(slot, carry):
            for n in range(CROWS // 64):
                rows = pl.ds(aligned(j * CROWS + n * 64, 64), 64)
                value = g2[slot, rows, :].astype(jnp.float32) * norm[slot, 0:1, :]
                lhs[slot, n * 64 : (n + 1) * 64, :] = value.astype(jnp.bfloat16)
            return carry

        lax.fori_loop(0, 16, step, 0)

    def multiply_normed(j):
        pbuf[1, j] = product(lhs, rb2, 0, 1 - zb).astype(jnp.bfloat16)
        partial_send(1, j).start()
        tq[j] = product(lhs, rb2, 0, zb)

    def finished(j):
        partial_send(1, j).wait_recv()

        def finish(n, carry):
            rows = pl.ds(aligned(n * 32, 32), 32)
            out[pl.ds(aligned(j * CROWS + n * 32, 32), 32), :] = (
                tq[j, rows, :] + prec[1, j, rows, :].astype(jnp.float32)
            ).astype(jnp.bfloat16)
            return carry

        lax.fori_loop(0, CROWS // 32, finish, 0, unroll=2)

    gather_far(1, g2, 0)
    normalize(0)
    coef_wait(1, rb2)
    multiply_normed(0)
    gather_near(1, g2, 2)
    gather_far(1, g2, 1)
    normalize(1)
    multiply_normed(1)
    finished(0)
    gather_far(1, g2, 2)
    normalize(2)
    multiply_normed(2)
    finished(1)
    finished(2)

    swap.wait_send()
    for j in range(CHUNKS):
        back(j).wait_send()
    for i, ext in ((0, oext), (1, dext)):
        for copy in rims(i, ext):
            copy.wait_send()
    for i, (g, r, rb) in enumerate(((g1, r1, rb1), (g2, r2, rb2))):
        gather_end(i, g)
        coef_end(i, r, rb)
        for j in range(CHUNKS):
            partial_send(i, j).wait_send()
    for step in range(1, 8):
        share(step).wait_send()
    for copy in norm_sends() + norm_forwards():
        copy.wait_send()


def shards(orbitals, potential, rot_first, rot_second):
    bf16, f32 = jnp.bfloat16, jnp.float32
    vmem = pl.BlockSpec(memory_space=pltpu.VMEM)
    dma = pltpu.SemaphoreType.DMA
    result = pl.pallas_call(
        kernel,
        out_shape=jax.ShapeDtypeStruct((ROWS, LANES), bf16),
        in_specs=[vmem] * 4,
        out_specs=vmem,
        scratch_shapes=[
            pltpu.VMEM((EXT * NY, HALF), bf16),
            pltpu.VMEM((EXT * NY, HALF), bf16),
            pltpu.VMEM((EXT, NY + 16, HALF), f32),
            pltpu.VMEM((GRID_X, NY), f32),
            pltpu.VMEM((PAIR, NY, HALF), f32),
            pltpu.VMEM((PAIR * NY, HALF), bf16),
            pltpu.VMEM((16, ROWS, LANES), bf16),
            pltpu.VMEM((16, ROWS, LANES), bf16),
            pltpu.VMEM((2, 4096, LANES), bf16),
            pltpu.VMEM((2, 4096, LANES), bf16),
            pltpu.VMEM((2, CHUNKS, CROWS, LANES), bf16),
            pltpu.VMEM((2, CHUNKS, CROWS, LANES), bf16),
            pltpu.VMEM((CHUNKS, CROWS, LANES), f32),
            pltpu.VMEM((8, 8, LANES), f32),
            pltpu.VMEM((16, 8, LANES), f32),
            pltpu.VMEM((16, CROWS, LANES), bf16),
            dma, dma,
            dma((CHUNKS,)), dma((CHUNKS,)),
            dma((1 + CHUNKS,)),
            dma((2, 2)), dma((2, 2)),
            dma((2, CHUNKS, 17)), dma((2, CHUNKS, 16)),
            dma((2, CHUNKS)), dma((2, CHUNKS)),
            dma((7,)), dma((7,)),
            dma((15,)), dma((16,)),
            dma((2, PIECES, 3)), dma((2, PIECES, 4)),
            dma((2, 2, PIECES, 4)), dma((2, 2, PIECES, 4)),
        ],
        compiler_params=pltpu.CompilerParams(
            collective_id=0, has_side_effects=True, vmem_limit_bytes=56 << 20
        ),
    )(orbitals.reshape(ROWS, LANES), potential, rot_first, rot_second)
    return result.reshape(OWN, NY, LANES)


def solution(mesh):
    placed = (P("dom", None, "band"), P(), P("dom", "band"), P("dom", "band"))
    return jax.shard_map(
        shards, mesh=mesh, in_specs=placed, out_specs=P("dom", None, "band"), check_vma=False
    )
```
